32 devices in a mesh: wide: 8 (over z, y), narrow: 4 (over x, core).
Axes of the slice: x: 2, y: 2, z: 4, core: 2. Of those that a mesh axis runs over, the one named last changes fastest.
Arguments:
- daily_fields: bfloat16 [256, 704, 1440], P('narrow', 'wide'), may hold values from -6 to 6
- order_table: int32 [384], replicated, may hold values from 0 to 383, as said below
- lag_days: int32 [3], replicated, may hold values from 1 to 8, as said below
- lag_weights: float32 [3, 384, 384, 2], P(None, 'narrow', 'wide'), may hold values from -0.5 to 0.5
Outputs:
- noise_variance: float32 [384, 384, 2], P('narrow', 'wide')
- covariance_panel: float32 [384, 12, 1536], P('wide', None, 'narrow')
The draws below stay inside these ranges and needn't reach their ends.
Inputs may be any that keep to these rules, and one draw needn't show every extreme that they name: `order_table`: slots 2k and 2k+1 hold the two orders m and 383 - m of one pair, the even one in slot 2k; every order appears once. `lag_days`: three different lags; one of them is 8.
All inputs are finite; a program needn't handle non-finite values.
Results may differ from the reference program's by a relative error of at most 0.0087.
Values may be sent and summed in bfloat16 or wider, within the bound.
No kernel may reach another device: no remote copies, remote signals or barrier semaphores. Data moves between devices by JAX's collectives and lax.ppermute only.
A program may use at most 128 MiB of HBM per device.

```python
import math
import jax
import jax.numpy as jnp
from jax import lax

NLAT = 704
NLON = 1440
M = 384
L = 384
T_DEV = 64
LAGMAX = 8
ROW_DEG = 3
TIMES = 256
DEG_DEV = 96
N_NARROW = 4


def draw_order_table(key, part):
    pair_order = jax.random.permutation(jax.random.fold_in(key, 11), M // 2).astype(jnp.int32)
    partner = M - 1 - pair_order
    even_member = jnp.where(pair_order % 2 == 0, pair_order, partner)
    odd_member = jnp.where(pair_order % 2 == 0, partner, pair_order)
    return jnp.stack([even_member, odd_member], axis=1).reshape(M).astype(jnp.int32)


def draw_lag_days(key, part):
    shorter = jax.random.permutation(jax.random.fold_in(key, 13), LAGMAX - 1)[:2].astype(jnp.int32) + 1
    picked = jnp.concatenate([shorter, jnp.array([LAGMAX], dtype=jnp.int32)])
    arrangement = jax.random.permutation(jax.random.fold_in(key, 17), 3)
    return picked[arrangement].astype(jnp.int32)


def steps_of(rng, shape, shards, low, high):
    def one(axis_at, blocks):
        heights = jax.random.uniform(jax.random.fold_in(jax.random.fold_in(rng, 6), axis_at), (blocks,), jnp.float32, low / len(shards), high / len(shards))
        return jnp.repeat(jnp.exp(heights), shape[axis_at] // blocks).reshape((-1,) + (1,) * (len(shape) - axis_at - 1))

    gain = one(*shards[0])
    for cut in shards[1:]:
        gain = gain * one(*cut)
    return gain


def normal_values(key, extent, deviation, limit, split=(), kind=jnp.bfloat16):
    result = jax.random.normal(key, extent, jnp.float32) * deviation
    if len(split) > 0:
        result = steps_of(key, extent, split, -0.22, 0.18) * result
    return jnp.clip(result, min=-limit, max=limit).astype(kind)


def setup_inputs(seed: int = 0) -> dict:
    splits = jax.random.split(jax.random.key(seed), 5)
    daily_fields = normal_values(splits[0], (TIMES, NLAT, NLON), 1.0, 6.0, ((0, 4), (1, 8)))
    order_table = draw_order_table(jax.random.fold_in(splits[4], 71), 0)
    lag_days = draw_lag_days(jax.random.fold_in(splits[4], 71), 0)
    lag_weights = jnp.clip(jax.random.uniform(splits[3], (3, L, M, 2), jnp.float32, -0.5, 0.5) * steps_of(splits[3], (3, L, M, 2), ((1, 4), (2, 8)), -0.4, 0.0), -0.5, 0.5)
    return dict(daily_fields=daily_fields, order_table=order_table, lag_days=lag_days, lag_weights=lag_weights)


def dft_table(order_table):
    longitude = jnp.arange(NLON, dtype=jnp.int32)
    phase_turns = order_table.astype(jnp.int32)[:, None] * longitude[None, :] % NLON
    angle = phase_turns.astype(jnp.float32) * (2.0 * math.pi / NLON)
    norm_scale = 1.0 / math.sqrt(NLON)
    return jnp.stack([jnp.cos(angle) * norm_scale, -jnp.sin(angle) * norm_scale], axis=1).astype(jnp.bfloat16)

def lat_basis():
    degree = jnp.arange(L, dtype=jnp.int32)
    odd_lat = 2 * jnp.arange(NLAT, dtype=jnp.int32) + 1
    period = 4 * NLAT
    even_turns = degree[:, None] * odd_lat[None, :] % period
    odd_turns = (degree[:, None] + 1) * odd_lat[None, :] % period
    angle_unit = math.pi / (2 * NLAT)
    norm_scale = math.sqrt(2.0 / NLAT)
    cosines = jnp.cos(even_turns.astype(jnp.float32) * angle_unit) * norm_scale
    sines = jnp.sin(odd_turns.astype(jnp.float32) * angle_unit) * norm_scale
    return jnp.stack([cosines, sines]).astype(jnp.bfloat16)

def reference(daily_fields, order_table, lag_days, lag_weights):
    dft_rows = dft_table(order_table).reshape(M * 2, NLON)
    lat_table = lat_basis()
    slot_basis = lat_table[order_table % 2].astype(jnp.float32)
    blocks = daily_fields.reshape(TIMES // T_DEV, T_DEV, NLAT, NLON)

    def transform(day_block):
        spectra = jnp.dot(day_block.reshape(T_DEV * NLAT, NLON), dft_rows.T, preferred_element_type=jnp.float32)
        spectra = spectra.astype(jnp.bfloat16).reshape(T_DEV, NLAT, M, 2)
        coeffs = jnp.einsum('slj,tjsc->lsct', slot_basis, spectra.astype(jnp.float32))
        return coeffs.astype(jnp.bfloat16)
    coeffs = lax.map(transform, blocks)
    coeffs = jnp.moveaxis(coeffs, 0, 3).reshape(L, M, 2, TIMES)
    day_index = jnp.arange(TIMES, dtype=jnp.int32)

    def degree_rows(inputs):
        series, weights = inputs
        series32 = series.astype(jnp.float32)
        residual = series32
        for position in range(3):
            shifted = jnp.roll(series32, lag_days[position], axis=-1)
            residual = residual - weights[position][..., None] * shifted
        residual = jnp.where(day_index >= LAGMAX, residual, 0.0)
        spread = lax.optimization_barrier(jnp.sum(residual * residual, axis=-1)) / (TIMES - LAGMAX)
        return (spread, residual[:, 0, :].astype(jnp.bfloat16))
    noise_variance, real_rows = lax.map(degree_rows, (coeffs, jnp.moveaxis(lag_weights, 0, 1)))
    pick_index = jnp.arange(ROW_DEG * N_NARROW, dtype=jnp.int32)
    row_degrees = pick_index // ROW_DEG * DEG_DEV + pick_index % ROW_DEG
    col_degrees = jnp.arange(N_NARROW, dtype=jnp.int32) * DEG_DEV + ROW_DEG
    row_series = real_rows[row_degrees].astype(jnp.float32)
    column_series = real_rows[col_degrees].astype(jnp.float32)
    cov_panel = jnp.einsum('jst,nqt->sjnq', row_series, column_series)
    cov_panel = cov_panel.reshape(M, ROW_DEG * N_NARROW, N_NARROW * M) / math.sqrt(TIMES - LAGMAX)
    return (noise_variance, cov_panel)
```

```python
import functools
import math

import jax
import jax.numpy as jnp
import numpy as np
from jax import lax
from jax.experimental import pallas as pl
from jax.experimental.pallas import tpu as pltpu
from jax.sharding import PartitionSpec as P

LAGMAX = 8
ROW_DEG = 3
VMEM = 48 * 2**20


def dft_parts(orders, longitudes):
    turns = np.arange(orders)[:, None] * np.arange(longitudes)[None, :] % longitudes
    angle = turns * (2.0 * np.pi / longitudes)
    scale = 1.0 / math.sqrt(longitudes)
    return np.stack([np.cos(angle) * scale, -np.sin(angle) * scale]).astype(jnp.bfloat16)


def lat_columns(degrees, latitudes):
    degree = np.arange(degrees)[None, :]
    odd_lat = 2 * np.arange(latitudes)[:, None] + 1
    period = 4 * latitudes
    unit = np.pi / (2 * latitudes)
    scale = math.sqrt(2.0 / latitudes)
    cosines = np.cos(degree * odd_lat % period * unit) * scale
    sines = np.sin((degree + 1) * odd_lat % period * unit) * scale
    return np.concatenate([cosines, sines], axis=1).astype(jnp.bfloat16)


def spectra_kernel(table_ref, field_ref, out_ref):
    out_ref[...] = lax.dot_general(
        table_ref[...],
        field_ref[...],
        (((1,), (1,)), ((), ())),
        preferred_element_type=jnp.float32,
    ).astype(jnp.bfloat16)


def spectra_of(table, fields, lat_local, day_block):
    rows, lon_count = table.shape
    cells = fields.shape[0]
    block = day_block * lat_local
    return pl.pallas_call(
        spectra_kernel,
        grid=(cells // block,),
        in_specs=[
            pl.BlockSpec((rows, lon_count), lambda i: (0, 0)),
            pl.BlockSpec((block, lon_count), lambda i: (i, 0)),
        ],
        out_specs=pl.BlockSpec((rows, block), lambda i: (0, i)),
        out_shape=jax.ShapeDtypeStruct((rows, cells), jnp.bfloat16),
        compiler_params=pltpu.CompilerParams(vmem_limit_bytes=VMEM),
        cost_estimate=pl.CostEstimate(
            flops=2 * rows * cells * lon_count,
            bytes_accessed=2 * (cells * lon_count + rows * cells + rows * lon_count),
            transcendentals=0,
        ),
    )(table, fields)


def coeffs_kernel(day_block, lat_local, recv_ref, lat_ref, out_ref, line_ref):
    sources, slots, _ = recv_ref.shape
    degrees = out_ref.shape[2]
    padded = line_ref.shape[1]
    for day in range(day_block):
        for source in range(sources):
            line_ref[day, :slots, source * lat_local : (source + 1) * lat_local] = recv_ref[
                source, :, day * lat_local : (day + 1) * lat_local
            ]
    both = jnp.dot(
        line_ref[...].reshape(day_block * padded, sources * lat_local),
        lat_ref[...],
        preferred_element_type=jnp.float32,
    ).reshape(day_block, padded, 2 * degrees)
    odd = lax.broadcasted_iota(jnp.int32, (day_block, padded, degrees), 1) % 2 == 1
    picked = jnp.where(odd, both[:, :, degrees:], both[:, :, :degrees])
    out_ref[...] = picked.astype(jnp.bfloat16)[:, :slots]


def coeffs_of(received, lat_table, days_local, day_block):
    sources, slots, cells = received.shape
    latitudes, degrees = lat_table.shape[0], lat_table.shape[1] // 2
    lat_local = latitudes // sources
    block = day_block * lat_local
    return pl.pallas_call(
        functools.partial(coeffs_kernel, day_block, lat_local),
        grid=(days_local // day_block,),
        in_specs=[
            pl.BlockSpec((sources, slots, block), lambda i: (0, 0, i)),
            pl.BlockSpec(lat_table.shape, lambda i: (0, 0)),
        ],
        out_specs=pl.BlockSpec((day_block, slots, degrees), lambda i: (i, 0, 0)),
        out_shape=jax.ShapeDtypeStruct((days_local, slots, degrees), jnp.bfloat16),
        scratch_shapes=[pltpu.VMEM((day_block, -(-slots // 16) * 16, latitudes), jnp.bfloat16)],
        compiler_params=pltpu.CompilerParams(vmem_limit_bytes=VMEM),
        cost_estimate=pl.CostEstimate(
            flops=4 * slots * cells * sources * degrees,
            bytes_accessed=2 * (sources * slots * cells + days_local * slots * degrees),
            transcendentals=0,
        ),
    )(received, lat_table)


def spread_kernel(lag_ref, series_ref, weight_ref, out_ref):
    days, slots, degrees = series_ref.shape
    step = 16 if slots % 16 == 0 else slots
    lags = [lag_ref[i] for i in range(3)]
    for first in range(0, slots, step):
        rows = pl.ds(first, step)
        weights = [weight_ref[i, rows, :] for i in range(3)]

        def add_day(day, total):
            residual = series_ref[day, rows, :].astype(jnp.float32)
            for lag, weight in zip(lags, weights):
                residual = residual - weight * series_ref[day - lag, rows, :].astype(jnp.float32)
            return total + residual * residual

        out_ref[rows, :] = lax.fori_loop(
            LAGMAX, days, add_day, jnp.zeros((step, degrees), jnp.float32), unroll=4
        )


def spread_of(lag_days, series, weights):
    days, slots, degrees = series.shape
    whole = pl.BlockSpec(memory_space=pltpu.VMEM)
    return pl.pallas_call(
        spread_kernel,
        in_specs=[pl.BlockSpec(memory_space=pltpu.SMEM), whole, whole],
        out_specs=whole,
        out_shape=jax.ShapeDtypeStruct((slots, degrees), jnp.float32),
        compiler_params=pltpu.CompilerParams(vmem_limit_bytes=VMEM),
        cost_estimate=pl.CostEstimate(
            flops=8 * days * slots * degrees,
            bytes_accessed=2 * days * slots * degrees + 16 * slots * degrees,
            transcendentals=0,
        ),
    )(lag_days, series, weights)


def swap_blocks(blocks, axis):
    count = lax.axis_size(axis)
    me = lax.axis_index(axis)
    got = [lax.dynamic_index_in_dim(blocks, me, 0, keepdims=False)]
    for hop in range(1, count):
        if count & (count - 1) == 0:
            target, pairs = me ^ hop, [(i, i ^ hop) for i in range(count)]
        else:
            target, pairs = (me + hop) % count, [(i, (i + hop) % count) for i in range(count)]
        block = lax.dynamic_index_in_dim(blocks, target, 0, keepdims=False)
        got.append(lax.ppermute(block, axis, pairs))
    order = jnp.arange(count, dtype=jnp.int32)
    order = (order ^ me) if count & (count - 1) == 0 else (me - order) % count
    return jnp.take(jnp.stack(got), order, axis=0)


def lagged_residual(series, weights, lag_days, days_axis, first, count):
    residual = lax.slice_in_dim(series, first, first + count, axis=days_axis).astype(jnp.float32)
    for position in range(3):
        shifted = lax.dynamic_slice_in_dim(
            series, first - lag_days[position], count, axis=days_axis
        )
        residual = residual - weights[position] * shifted.astype(jnp.float32)
    return residual


def body(daily_fields, order_table, lag_days, lag_weights):
    wide_count = lax.axis_size("wide")
    narrow_count = lax.axis_size("narrow")
    days_local, lat_local, lon_count = daily_fields.shape
    order_count = order_table.shape[0]
    slot_local = order_count // wide_count
    deg_local = lag_weights.shape[1]
    deg_count = deg_local * narrow_count
    times_all = days_local * narrow_count
    kept_days = times_all - LAGMAX
    day_block = math.gcd(128 // math.gcd(128, lat_local), days_local)

    fields = daily_fields.reshape(days_local * lat_local, lon_count)
    parts = jnp.asarray(dft_parts(order_count, lon_count))
    lat_table = jnp.asarray(lat_columns(deg_count, lat_local * wide_count))
    by_owner = order_table.reshape(wide_count, slot_local)

    if slot_local % 16 == 0 and slot_local > 16:
        chunks = [(0, 0, 16), (0, 16, slot_local), (1, 0, slot_local - 16), (1, slot_local - 16, slot_local)]
    else:
        chunks = [(0, 0, slot_local), (1, 0, slot_local)]

    own_weights = jnp.transpose(lag_weights, (3, 0, 2, 1))
    all_weights = lax.all_gather(own_weights, "narrow", axis=3, tiled=True)

    series = []
    spreads = []
    for part, first, last in chunks:
        count = last - first
        orders = by_owner[:, first:last].reshape(wide_count * count)
        pick = (orders[:, None] == jnp.arange(order_count, dtype=jnp.int32)[None, :]).astype(
            jnp.bfloat16
        )
        table = jnp.dot(pick, parts[part], preferred_element_type=jnp.float32).astype(jnp.bfloat16)
        spectra = spectra_of(table, fields, lat_local, day_block)
        spectra = spectra.reshape(wide_count, count, days_local * lat_local)
        received = lax.all_to_all(spectra, "wide", split_axis=0, concat_axis=0, tiled=True)
        coeffs = coeffs_of(received, lat_table, days_local, day_block)
        series.append((part, coeffs))
        inner = spread_of(lag_days, coeffs, all_weights[part, :, first:last])
        ends = jnp.concatenate([coeffs[:LAGMAX], coeffs[days_local - LAGMAX :]], axis=0)
        ends = jnp.transpose(
            ends.reshape(2 * LAGMAX, count, narrow_count, deg_local), (2, 0, 1, 3)
        )
        inner = jnp.transpose(inner.reshape(count, narrow_count, deg_local), (1, 0, 2))
        ends = swap_blocks(ends, "narrow")
        inner = swap_blocks(inner, "narrow")
        seams = jnp.concatenate([ends[:-1, LAGMAX:], ends[1:, :LAGMAX]], axis=1)
        seam = lagged_residual(
            seams, own_weights[part, :, first:last], lag_days, 1, LAGMAX, LAGMAX
        )
        spreads.append(jnp.sum(inner, axis=0) + jnp.sum(seam * seam, axis=(0, 1)))

    split = [sum(1 for p, _, _ in chunks if p == 0)]
    spread = jnp.stack(
        [jnp.concatenate(spreads[: split[0]], axis=0), jnp.concatenate(spreads[split[0] :], axis=0)],
        axis=2,
    )
    noise_variance = jnp.transpose(spread / kept_days, (1, 0, 2))

    picked = []
    for part, coeffs in series:
        if part == 0:
            by_block = coeffs.reshape(days_local, coeffs.shape[1], narrow_count, deg_local)
            picked.append(by_block[..., : ROW_DEG + 1])
    picked = jnp.transpose(jnp.concatenate(picked, axis=1), (1, 2, 3, 0))
    picked = lax.all_gather(picked, "narrow", axis=3, tiled=True)
    panel_weights = all_weights[0].reshape(3, slot_local, narrow_count, deg_local)
    panel_weights = panel_weights[..., : ROW_DEG + 1, None]
    kept = lagged_residual(picked, panel_weights, lag_days, 3, LAGMAX, kept_days)
    kept = kept.astype(jnp.bfloat16)
    rows = kept[:, :, :ROW_DEG].reshape(slot_local, narrow_count * ROW_DEG, kept_days)
    column = lax.dynamic_index_in_dim(kept[:, :, ROW_DEG], lax.axis_index("narrow"), 1, False)
    columns = lax.all_gather(column, "wide", axis=0, tiled=True)
    panel = lax.dot_general(
        rows, columns, (((2,), (1,)), ((), ())), preferred_element_type=jnp.float32
    )
    return (noise_variance, panel / math.sqrt(kept_days))


def solution(mesh):
    placed = (P("narrow", "wide", None), P(), P(), P(None, "narrow", "wide", None))
    return jax.shard_map(
        body,
        mesh=mesh,
        in_specs=placed,
        out_specs=(P("narrow", "wide", None), P("wide", None, "narrow")),
        check_vma=False,
    )
```

```python
import functools
import math

import jax
import jax.numpy as jnp
import numpy as np
from jax import lax
from jax.experimental import pallas as pl
from jax.experimental.pallas import tpu as pltpu
from jax.sharding import PartitionSpec as P

LAGMAX = 8
ROW_DEG = 3
VMEM = 48 * 2**20


def dft_columns(orders, longitudes):
    turns = np.arange(longitudes)[:, None] * np.arange(orders)[None, :] % longitudes
    angle = turns * (2.0 * np.pi / longitudes)
    scale = 1.0 / math.sqrt(longitudes)
    return [(np.cos(angle) * scale).astype(jnp.bfloat16), (-np.sin(angle) * scale).astype(jnp.bfloat16)]


def lat_columns(degrees, latitudes):
    degree = np.arange(degrees)[None, :]
    odd_lat = 2 * np.arange(latitudes)[:, None] + 1
    period = 4 * latitudes
    unit = np.pi / (2 * latitudes)
    scale = math.sqrt(2.0 / latitudes)
    cosines = np.cos(degree * odd_lat % period * unit) * scale
    sines = np.sin((degree + 1) * odd_lat % period * unit) * scale
    return np.concatenate([cosines, sines], axis=1).astype(jnp.bfloat16)


ANY = pl.BlockSpec(memory_space=pl.ANY)
IN_VMEM = pl.BlockSpec(memory_space=pltpu.VMEM)
IN_SMEM = pl.BlockSpec(memory_space=pltpu.SMEM)


def spectra_kernel(field_ref, table_ref, *refs):
    out_ref = refs[-1]
    cells = jnp.dot(field_ref[...], table_ref[...], preferred_element_type=jnp.float32)
    out_ref[...] = cells.T.astype(jnp.bfloat16)


def spectra_of(fields, table, block, after):
    cells, lon_count = fields.shape
    rows = table.shape[1]
    return pl.pallas_call(
        spectra_kernel,
        grid=(cells // block,),
        in_specs=[
            pl.BlockSpec((block, lon_count), lambda i: (i, 0)),
            pl.BlockSpec((lon_count, rows), lambda i: (0, 0)),
        ]
        + [ANY] * len(after),
        out_specs=pl.BlockSpec((rows, block), lambda i: (0, i)),
        out_shape=jax.ShapeDtypeStruct((rows, cells), jnp.bfloat16),
        compiler_params=pltpu.CompilerParams(vmem_limit_bytes=VMEM),
        cost_estimate=pl.CostEstimate(
            flops=2 * rows * cells * lon_count,
            bytes_accessed=2 * (cells * lon_count + rows * cells + rows * lon_count),
            transcendentals=0,
        ),
    )(fields, table, *after)


def peer(me, hop, count):
    if count & (count - 1) == 0:
        return me ^ hop, me ^ hop
    return (me + hop) % count, (me - hop + count) % count


def digest_kernel(shape, lag_ref, me_ref, recv_ref, lat_ref, weight_ref, *refs):
    narrow_count, lat_local, n_after = shape
    sends, pick_ref = refs[n_after : n_after + narrow_count], refs[n_after + narrow_count]
    line_ref, series_ref, block_ref = refs[n_after + narrow_count + 1 :]
    sources, slots, _ = recv_ref.shape
    days, _, degrees = series_ref.shape
    half, padded = slots // 2, line_ref.shape[1] // 2
    for day in range(days):
        for source in range(sources):
            block = recv_ref[source, :, day * lat_local : (day + 1) * lat_local]
            lats = slice(source * lat_local, (source + 1) * lat_local)
            if half == padded:
                line_ref[day, :, lats] = block
            else:
                line_ref[day, :half, lats] = block[:half]
                line_ref[day, padded : padded + half, lats] = block[half:]
    for parity in range(2):
        lines = line_ref[:, parity * padded : (parity + 1) * padded, :]
        coeffs = jnp.dot(
            lines.reshape(days * padded, sources * lat_local),
            lat_ref[:, parity * degrees : (parity + 1) * degrees],
            preferred_element_type=jnp.float32,
        )
        coeffs = coeffs.astype(jnp.bfloat16).reshape(days, padded, degrees)
        series_ref[:, parity * half : (parity + 1) * half, :] = coeffs[:, :half]

    step = 16 if slots % 16 == 0 else slots
    lags = [lag_ref[i] for i in range(3)]
    deg_local = degrees // narrow_count
    for first in range(0, slots, step):
        rows = pl.ds(first, step)
        weights = [weight_ref[i, rows, :] for i in range(3)]

        def add_day(day, total):
            residual = series_ref[day, rows, :].astype(jnp.float32)
            for lag, weight in zip(lags, weights):
                residual = residual - weight * series_ref[day - lag, rows, :].astype(jnp.float32)
            return total + residual * residual

        total = lax.fori_loop(
            LAGMAX, days, add_day, jnp.zeros((step, degrees), jnp.float32), unroll=4
        )
        coarse = total.astype(jnp.bfloat16)
        fine = (total - coarse.astype(jnp.float32)).astype(jnp.bfloat16)
        for owner in range(narrow_count):
            own = slice(owner * deg_local, (owner + 1) * deg_local)
            block_ref[owner, :LAGMAX, rows, :] = series_ref[:LAGMAX, rows, own]
            block_ref[owner, LAGMAX : 2 * LAGMAX, rows, :] = series_ref[days - LAGMAX :, rows, own]
            block_ref[owner, 2 * LAGMAX, rows, :] = coarse[:, own]
            block_ref[owner, 2 * LAGMAX + 1, rows, :] = fine[:, own]
    for owner in range(narrow_count):
        kept = slice(owner * (ROW_DEG + 1), (owner + 1) * (ROW_DEG + 1))
        first = owner * deg_local
        pick_ref[:, :, kept] = series_ref[:, :, first : first + ROW_DEG + 1]
    me = me_ref[0]
    for hop, send in enumerate(sends):
        send[...] = block_ref[peer(me, hop, narrow_count)[0]]


def digest(lag_days, me, received, lat_table, weights, days_local, narrow_count, after):
    sources, slots, cells = received.shape
    latitudes, degrees = lat_table.shape[0], lat_table.shape[1] // 2
    lat_local = latitudes // sources
    deg_local = degrees // narrow_count
    padded = 2 * (-(-(slots // 2) // 8) * 8)
    message = (2 * LAGMAX + 2, slots, deg_local)
    picked = (days_local, slots, narrow_count * (ROW_DEG + 1))
    return pl.pallas_call(
        functools.partial(digest_kernel, (narrow_count, lat_local, len(after))),
        in_specs=[IN_SMEM, IN_SMEM, IN_VMEM, IN_VMEM, IN_VMEM] + [ANY] * len(after),
        out_specs=[IN_VMEM] * (narrow_count + 1),
        out_shape=[jax.ShapeDtypeStruct(message, jnp.bfloat16)] * narrow_count
        + [jax.ShapeDtypeStruct(picked, jnp.bfloat16)],
        scratch_shapes=[
            pltpu.VMEM((days_local, padded, latitudes), jnp.bfloat16),
            pltpu.VMEM((days_local, slots, degrees), jnp.bfloat16),
            pltpu.VMEM((narrow_count,) + message, jnp.bfloat16),
        ],
        compiler_params=pltpu.CompilerParams(vmem_limit_bytes=VMEM),
        cost_estimate=pl.CostEstimate(
            flops=4 * slots * cells * sources * degrees,
            bytes_accessed=2 * (sources * slots * cells + days_local * slots * degrees),
            transcendentals=0,
        ),
    )(lag_days, me, received, lat_table, weights, *after)


def combine_kernel(count, lag_ref, me_ref, weight_ref, *refs):
    got, out_ref, seam_ref, sum_ref = refs[:count], refs[count], refs[count + 1], refs[count + 2]
    me = me_ref[0]
    total = jnp.zeros(out_ref.shape, jnp.float32)
    for hop in range(count):
        source = peer(me, hop, count)[1]
        seam_ref[source, LAGMAX:] = got[hop][:LAGMAX]
        seam_ref[source + 1, :LAGMAX] = got[hop][LAGMAX : 2 * LAGMAX]
        sums = got[hop][2 * LAGMAX :].astype(jnp.float32)
        sum_ref[source] = sums[0] + sums[1]
    for source in range(count):
        total = total + sum_ref[source]
    lags = [lag_ref[i] for i in range(3)]
    weights = [weight_ref[i] for i in range(3)]
    for block in range(1, count):
        for day in range(LAGMAX, 2 * LAGMAX):
            residual = seam_ref[block, day].astype(jnp.float32)
            for lag, weight in zip(lags, weights):
                residual = residual - weight * seam_ref[block, day - lag].astype(jnp.float32)
            total = total + residual * residual
    out_ref[...] = total


def combine(lag_days, me, weights, got):
    count = len(got)
    days, slots, degrees = got[0].shape
    return pl.pallas_call(
        functools.partial(combine_kernel, count),
        in_specs=[IN_SMEM, IN_SMEM] + [IN_VMEM] * (count + 1),
        out_specs=IN_VMEM,
        out_shape=jax.ShapeDtypeStruct((slots, degrees), jnp.float32),
        scratch_shapes=[
            pltpu.VMEM((count + 1, 2 * LAGMAX, slots, degrees), jnp.bfloat16),
            pltpu.VMEM((count, slots, degrees), jnp.float32),
        ],
        compiler_params=pltpu.CompilerParams(vmem_limit_bytes=VMEM),
        cost_estimate=pl.CostEstimate(
            flops=8 * count * LAGMAX * slots * degrees,
            bytes_accessed=2 * count * days * slots * degrees,
            transcendentals=0,
        ),
    )(lag_days, me, weights, *got)


def swap(sends, axis):
    count = lax.axis_size(axis)
    return [sends[0]] + [
        lax.ppermute(sends[hop], axis, [(i, peer(i, hop, count)[0]) for i in range(count)])
        for hop in range(1, count)
    ]


def by_source(got, axis):
    count = lax.axis_size(axis)
    me = lax.axis_index(axis)
    hops = jnp.arange(count, dtype=jnp.int32)
    hops = hops ^ me if count & (count - 1) == 0 else (me - hops + count) % count
    return jnp.take(jnp.stack(got), hops, axis=0)


def segments_of(slot_local):
    pairs = slot_local // 2
    if slot_local % 48 == 0:
        cut = pairs * 2 // 3
        return [[(0, 0, cut)], [(0, cut, pairs), (1, 0, cut)], [(1, cut, pairs)]]
    return [[(0, 0, pairs)], [(1, 0, pairs)]]


def body(daily_fields, order_table, lag_days, lag_weights):
    wide_count = lax.axis_size("wide")
    narrow_count = lax.axis_size("narrow")
    days_local, lat_local, lon_count = daily_fields.shape
    order_count = order_table.shape[0]
    slot_local = order_count // wide_count
    pair_local = slot_local // 2
    deg_local = lag_weights.shape[1]
    deg_count = deg_local * narrow_count
    kept_days = days_local * narrow_count - LAGMAX
    day_block = math.gcd(128 // math.gcd(128, lat_local), days_local)
    me = lax.axis_index("narrow").astype(jnp.int32).reshape(1)

    fields = daily_fields.reshape(days_local * lat_local, lon_count)
    parts = [jnp.asarray(p) for p in dft_columns(order_count, lon_count)]
    lat_table = jnp.asarray(lat_columns(deg_count, lat_local * wide_count))
    by_owner = order_table.reshape(wide_count, pair_local, 2)
    every_order = jnp.arange(order_count, dtype=jnp.int32)[:, None]

    def table_of(segments):
        columns = []
        for parity in range(2):
            for part, first, last in segments:
                orders = by_owner[:, first:last, parity]
                columns.append((part, orders))
        picks = []
        for part in range(2):
            if any(p == part for p, _ in columns):
                chosen = jnp.concatenate(
                    [orders if p == part else jnp.full_like(orders, -1) for p, orders in columns], axis=1
                ).reshape(1, -1)
                picks.append(
                    jnp.dot(
                        parts[part],
                        (every_order == chosen).astype(jnp.bfloat16),
                        preferred_element_type=jnp.float32,
                    )
                )
        return sum(picks[1:], picks[0]).astype(jnp.bfloat16)

    own_weights = jnp.transpose(
        lag_weights.reshape(3, deg_local, pair_local, 2, 2), (4, 3, 0, 2, 1)
    )
    all_weights = by_source(swap([own_weights] * narrow_count, "narrow"), "narrow")
    all_weights = jnp.moveaxis(all_weights, 0, 4).reshape(2, 2, 3, pair_local, deg_count)

    def rows_of(weights, segments):
        return jnp.concatenate(
            [weights[p, parity, :, a:b] for parity in range(2) for p, a, b in segments], axis=1
        )

    plan = segments_of(slot_local)
    spreads = {}
    picked = {}
    results = []
    received = []
    panel = None

    def exchange(segments, after):
        spectra = spectra_of(fields, table_of(segments), day_block * lat_local, after)
        spectra = spectra.reshape(wide_count, -1, days_local * lat_local)
        return lax.all_to_all(spectra, "wide", split_axis=0, concat_axis=0, tiled=True)

    def finish(segments, received, after):
        *sends, picks = digest(
            lag_days,
            me,
            received,
            lat_table,
            rows_of(all_weights, segments),
            days_local,
            narrow_count,
            after,
        )
        total = combine(lag_days, me, rows_of(own_weights, segments), swap(sends, "narrow"))
        at = 0
        for parity in range(2):
            for part, first, last in segments:
                rows = slice(at, at + last - first)
                spreads[part, parity, first] = total[rows]
                if part == 0:
                    picked[parity, first] = picks[:, rows]
                at += last - first
        return total

    def panel_of():
        series = jnp.stack(
            [
                jnp.concatenate([picked[k] for k in sorted(picked) if k[0] == parity], axis=1)
                for parity in range(2)
            ],
            axis=2,
        )
        series = series.reshape(days_local, slot_local, narrow_count * (ROW_DEG + 1))
        series = jnp.transpose(series, (1, 2, 0))
        series = by_source(swap([series] * narrow_count, "narrow"), "narrow")
        series = jnp.moveaxis(series, 0, 2).reshape(
            slot_local, narrow_count, ROW_DEG + 1, days_local * narrow_count
        )
        weights = all_weights[0].reshape(2, 3, pair_local, narrow_count, deg_local)
        weights = jnp.transpose(weights[..., : ROW_DEG + 1], (1, 2, 0, 3, 4)).reshape(
            3, slot_local, narrow_count, ROW_DEG + 1, 1
        )
        residual = series[..., LAGMAX:].astype(jnp.float32)
        for position in range(3):
            shifted = lax.dynamic_slice_in_dim(series, LAGMAX - lag_days[position], kept_days, axis=3)
            residual = residual - weights[position] * shifted.astype(jnp.float32)
        rounded = residual.astype(jnp.bfloat16)
        rows = rounded[:, :, :ROW_DEG].reshape(slot_local, narrow_count * ROW_DEG, kept_days)
        column = lax.dynamic_index_in_dim(rounded[:, :, ROW_DEG], me[0], 1, False)
        columns = by_source(swap([column] * wide_count, "wide"), "wide")
        columns = columns.reshape(order_count, kept_days)
        product = lax.dot_general(
            rows, columns, (((2,), (1,)), ((), ())), preferred_element_type=jnp.float32
        )
        return product / math.sqrt(kept_days)

    for index, segments in enumerate(plan):
        if index >= 2:
            results.append(finish(plan[index - 2], received[index - 2], results[-1:]))
        received.append(exchange(segments, results[-1:]))
    results.append(finish(plan[-2], received[-2], results[-1:]))
    panel = panel_of()
    finish(plan[-1], received[-1], results[-1:] + [panel])

    spread = jnp.stack(
        [
            jnp.stack(
                [
                    jnp.concatenate(
                        [spreads[k] for k in sorted(spreads) if k[:2] == (part, parity)], axis=0
                    )
                    for part in range(2)
                ]
            )
            for parity in range(2)
        ]
    )
    noise_variance = jnp.transpose(spread / kept_days, (3, 2, 0, 1)).reshape(deg_local, slot_local, 2)
    return (noise_variance, panel)


def solution(mesh):
    placed = (P("narrow", "wide", None), P(), P(), P(None, "narrow", "wide", None))
    return jax.shard_map(
        body,
        mesh=mesh,
        in_specs=placed,
        out_specs=(P("narrow", "wide", None), P("wide", None, "narrow")),
        check_vma=False,
    )
```

```python
import functools
import math

import jax
import jax.numpy as jnp
import numpy as np
from jax import lax
from jax.experimental import pallas as pl
from jax.experimental.pallas import tpu as pltpu
from jax.sharding import PartitionSpec as P

LAGMAX = 8
ROW_DEG = 3
VMEM = 48 * 2**20


def dft_columns(orders, longitudes):
    turns = np.arange(longitudes)[:, None] * np.arange(orders)[None, :] % longitudes
    angle = turns * (2.0 * np.pi / longitudes)
    scale = 1.0 / math.sqrt(longitudes)
    return [(np.cos(angle) * scale).astype(jnp.bfloat16), (-np.sin(angle) * scale).astype(jnp.bfloat16)]


def lat_columns(degrees, latitudes):
    degree = np.arange(degrees)[None, :]
    odd_lat = 2 * np.arange(latitudes)[:, None] + 1
    period = 4 * latitudes
    unit = np.pi / (2 * latitudes)
    scale = math.sqrt(2.0 / latitudes)
    cosines = np.cos(degree * odd_lat % period * unit) * scale
    sines = np.sin((degree + 1) * odd_lat % period * unit) * scale
    return np.concatenate([cosines, sines], axis=1).astype(jnp.bfloat16)


ANY = pl.BlockSpec(memory_space=pl.ANY)
IN_HBM = pl.BlockSpec(memory_space=pltpu.HBM)
IN_VMEM = pl.BlockSpec(memory_space=pltpu.VMEM)
IN_SMEM = pl.BlockSpec(memory_space=pltpu.SMEM)


def table_from(owned, order_ref, part):
    slot_local, first, last = owned
    slots = order_ref.shape[1]
    held = last - first
    rows = slots // slot_local * 2 * held
    column = lax.broadcasted_iota(jnp.int32, (1, rows), 1)
    owner, place = lax.div(column, 2 * held), lax.rem(column, 2 * held)
    odd = (place >= held).astype(jnp.int32)
    slot = owner * slot_local + 2 * (first + place - held * odd) + odd
    here = lax.broadcasted_iota(jnp.int32, (slots, rows), 0)
    orders = jnp.broadcast_to(order_ref[...].astype(jnp.float32), (8, slots))
    chosen = jnp.dot(
        orders,
        (here == slot).astype(jnp.float32),
        precision=lax.Precision.HIGHEST,
        preferred_element_type=jnp.float32,
    )
    picks = (here.astype(jnp.float32) == chosen[:1]).astype(jnp.bfloat16)
    return jnp.dot(part, picks, preferred_element_type=jnp.float32).astype(jnp.bfloat16)


def spectra_kernel(owned, order_ref, part_ref, field_ref, *refs):
    out_ref, table_ref = refs[-2:]

    @pl.when(pl.program_id(0) == 0)
    def _():
        table_ref[...] = table_from(owned, order_ref, part_ref[...])

    cells = jnp.dot(field_ref[...], table_ref[...], preferred_element_type=jnp.float32)
    out_ref[...] = cells.T.astype(jnp.bfloat16)


def first_spectra_kernel(owned, order_ref, part_hbm, field_hbm, out_ref, part_ref, field_ref, sems):
    block = out_ref.shape[1]
    cut = block // 256 * 128
    pieces = [(0, cut), (cut, block)]
    copies = [pltpu.make_async_copy(part_hbm, part_ref, sems.at[0])]
    for index, (start, stop) in enumerate(pieces):
        rows = pl.ds(start, stop - start)
        copies.append(
            pltpu.make_async_copy(field_hbm.at[rows], field_ref.at[rows], sems.at[index + 1])
        )
    for copy in copies:
        copy.start()
    copies[0].wait()
    table = table_from(owned, order_ref, part_ref[...])
    for (start, stop), copy in zip(pieces, copies[1:]):
        copy.wait()
        cells = jnp.dot(field_ref[start:stop], table, preferred_element_type=jnp.float32)
        out_ref[:, start:stop] = cells.T.astype(jnp.bfloat16)


def spectra_of(order_row, owned, part, fields, block, blocks, after):
    lon_count = fields.shape[1]
    first, last = blocks
    slot_local, first_pair, last_pair = owned
    rows = order_row.shape[1] // slot_local * 2 * (last_pair - first_pair)
    cells = (last - first) * block
    alone = blocks == (0, 1) and block % 128 == 0 and block > 128 and not after
    cost = pl.CostEstimate(
        flops=2 * rows * cells * lon_count,
        bytes_accessed=2 * (cells * lon_count + rows * (cells + lon_count)),
        transcendentals=0,
    )
    out_shape = jax.ShapeDtypeStruct((rows, cells), jnp.bfloat16)
    params = pltpu.CompilerParams(vmem_limit_bytes=VMEM)
    if alone:
        return pl.pallas_call(
            functools.partial(first_spectra_kernel, owned),
            in_specs=[IN_VMEM, IN_HBM, IN_HBM],
            out_specs=IN_VMEM,
            out_shape=out_shape,
            scratch_shapes=[
                pltpu.VMEM(part.shape, jnp.bfloat16),
                pltpu.VMEM((block, lon_count), jnp.bfloat16),
                pltpu.SemaphoreType.DMA((3,)),
            ],
            compiler_params=params,
            cost_estimate=cost,
        )(order_row, part, fields)
    return pl.pallas_call(
        functools.partial(spectra_kernel, owned),
        grid=(last - first,),
        in_specs=[
            pl.BlockSpec(order_row.shape, lambda i: (0, 0)),
            pl.BlockSpec(part.shape, lambda i: (0, 0)),
            pl.BlockSpec((block, lon_count), lambda i: (i + first, 0)),
        ]
        + [ANY] * len(after),
        out_specs=pl.BlockSpec((rows, block), lambda i: (0, i)),
        out_shape=out_shape,
        scratch_shapes=[pltpu.VMEM((lon_count, rows), jnp.bfloat16)],
        compiler_params=params,
        cost_estimate=cost,
    )(order_row, part, fields, *after)


def peer(me, hop, count):
    if count & (count - 1) == 0:
        return me ^ hop, me ^ hop
    return (me + hop) % count, (me - hop + count) % count


def digest_kernel(shape, lag_ref, me_ref, weight_ref, lat_hbm, *refs):
    groups, narrow_count, lat_local, n_after = shape
    blocks, refs = refs[:groups], refs[groups + n_after :]
    lat_ref, lat_sem = refs[-2:]
    refs = refs[:-2]
    lat_copy = pltpu.make_async_copy(lat_hbm, lat_ref, lat_sem)
    lat_copy.start()
    sends, pick_ref = refs[:narrow_count], refs[narrow_count]
    line_ref, series_ref, block_ref = refs[narrow_count + 1 :]
    days, slots, degrees = series_ref.shape
    half, padded = slots // 2, line_ref.shape[1] // 2
    start = 0
    for block in blocks:
        stop = start + block.shape[2] // lat_local
        for day in range(start, stop):
            cells = slice((day - start) * lat_local, (day - start + 1) * lat_local)
            for source in range(block.shape[0]):
                lats = slice(source * lat_local, (source + 1) * lat_local)
                if half == padded:
                    line_ref[day, :, lats] = block[source, :, cells]
                else:
                    line_ref[day, :half, lats] = block[source, :half, cells]
                    line_ref[day, padded : padded + half, lats] = block[source, half:, cells]
        if start == 0:
            lat_copy.wait()
        for parity in range(2):
            lines = line_ref[start:stop, parity * padded : (parity + 1) * padded, :]
            coeffs = jnp.dot(
                lines.reshape((stop - start) * padded, lat_ref.shape[0]),
                lat_ref[:, parity * degrees : (parity + 1) * degrees],
                preferred_element_type=jnp.float32,
            )
            coeffs = coeffs.astype(jnp.bfloat16).reshape(stop - start, padded, degrees)
            series_ref[start:stop, parity * half : (parity + 1) * half, :] = coeffs[:, :half]
        start = stop

    step = 16 if slots % 16 == 0 else slots
    lags = [lag_ref[i] for i in range(3)]
    deg_local = degrees // narrow_count
    for first in range(0, slots, step):
        rows = pl.ds(first, step)
        weights = [weight_ref[i, rows, :] for i in range(3)]

        def add_day(day, total):
            residual = series_ref[day, rows, :].astype(jnp.float32)
            for lag, weight in zip(lags, weights):
                residual = residual - weight * series_ref[day - lag, rows, :].astype(jnp.float32)
            return total + residual * residual

        total = lax.fori_loop(
            LAGMAX, days, add_day, jnp.zeros((step, degrees), jnp.float32), unroll=4
        )
        coarse = total.astype(jnp.bfloat16)
        fine = (total - coarse.astype(jnp.float32)).astype(jnp.bfloat16)
        for owner in range(narrow_count):
            own = slice(owner * deg_local, (owner + 1) * deg_local)
            block_ref[owner, :LAGMAX, rows, :] = series_ref[:LAGMAX, rows, own]
            block_ref[owner, LAGMAX : 2 * LAGMAX, rows, :] = series_ref[days - LAGMAX :, rows, own]
            block_ref[owner, 2 * LAGMAX, rows, :] = coarse[:, own]
            block_ref[owner, 2 * LAGMAX + 1, rows, :] = fine[:, own]
    for owner in range(narrow_count):
        kept = slice(owner * (ROW_DEG + 1), (owner + 1) * (ROW_DEG + 1))
        first = owner * deg_local
        pick_ref[:, :, kept] = series_ref[:, :, first : first + ROW_DEG + 1]
    me = me_ref[0]
    for hop, send in enumerate(sends):
        send[...] = block_ref[peer(me, hop, narrow_count)[0]]


def digest(lag_days, me, received, lat_table, weights, narrow_count, after):
    sources, slots, _ = received[0].shape
    latitudes, degrees = lat_table.shape[0], lat_table.shape[1] // 2
    lat_local = latitudes // sources
    days_local = sum(block.shape[2] for block in received) // lat_local
    deg_local = degrees // narrow_count
    padded = 2 * (-(-(slots // 2) // 8) * 8)
    message = (2 * LAGMAX + 2, slots, deg_local)
    picked = (days_local, slots, narrow_count * (ROW_DEG + 1))
    return pl.pallas_call(
        functools.partial(digest_kernel, (len(received), narrow_count, lat_local, len(after))),
        in_specs=[IN_SMEM, IN_SMEM, IN_VMEM, IN_HBM] + [IN_VMEM] * len(received) + [ANY] * len(after),
        out_specs=[IN_VMEM] * (narrow_count + 1),
        out_shape=[jax.ShapeDtypeStruct(message, jnp.bfloat16)] * narrow_count
        + [jax.ShapeDtypeStruct(picked, jnp.bfloat16)],
        scratch_shapes=[
            pltpu.VMEM((days_local, padded, latitudes), jnp.bfloat16),
            pltpu.VMEM((days_local, slots, degrees), jnp.bfloat16),
            pltpu.VMEM((narrow_count,) + message, jnp.bfloat16),
            pltpu.VMEM(lat_table.shape, jnp.bfloat16),
            pltpu.SemaphoreType.DMA(()),
        ],
        compiler_params=pltpu.CompilerParams(vmem_limit_bytes=VMEM),
        cost_estimate=pl.CostEstimate(
            flops=4 * slots * days_local * latitudes * degrees,
            bytes_accessed=2 * slots * days_local * (latitudes + degrees),
            transcendentals=0,
        ),
    )(lag_days, me, weights, lat_table, *received, *after)


def tie(array, after):
    return pl.pallas_call(
        lambda *refs: None,
        in_specs=[ANY] * (1 + len(after)),
        out_specs=ANY,
        out_shape=jax.ShapeDtypeStruct(array.shape, array.dtype),
        input_output_aliases={0: 0},
    )(array, *after)


def combine_kernel(count, lag_ref, me_ref, weight_ref, *refs):
    got, out_ref, seam_ref, sum_ref = refs[:count], refs[count], refs[count + 1], refs[count + 2]
    me = me_ref[0]
    total = jnp.zeros(out_ref.shape, jnp.float32)
    for hop in range(count):
        source = peer(me, hop, count)[1]
        seam_ref[source, LAGMAX:] = got[hop][:LAGMAX]
        seam_ref[source + 1, :LAGMAX] = got[hop][LAGMAX : 2 * LAGMAX]
        sums = got[hop][2 * LAGMAX :].astype(jnp.float32)
        sum_ref[source] = sums[0] + sums[1]
    for source in range(count):
        total = total + sum_ref[source]
    lags = [lag_ref[i] for i in range(3)]
    weights = [weight_ref[i] for i in range(3)]
    for block in range(1, count):
        for day in range(LAGMAX, 2 * LAGMAX):
            residual = seam_ref[block, day].astype(jnp.float32)
            for lag, weight in zip(lags, weights):
                residual = residual - weight * seam_ref[block, day - lag].astype(jnp.float32)
            total = total + residual * residual
    out_ref[...] = total


def combine(lag_days, me, weights, got):
    count = len(got)
    days, slots, degrees = got[0].shape
    return pl.pallas_call(
        functools.partial(combine_kernel, count),
        in_specs=[IN_SMEM, IN_SMEM] + [IN_VMEM] * (count + 1),
        out_specs=IN_VMEM,
        out_shape=jax.ShapeDtypeStruct((slots, degrees), jnp.float32),
        scratch_shapes=[
            pltpu.VMEM((count + 1, 2 * LAGMAX, slots, degrees), jnp.bfloat16),
            pltpu.VMEM((count, slots, degrees), jnp.float32),
        ],
        compiler_params=pltpu.CompilerParams(vmem_limit_bytes=VMEM),
        cost_estimate=pl.CostEstimate(
            flops=8 * count * LAGMAX * slots * degrees,
            bytes_accessed=2 * count * days * slots * degrees,
            transcendentals=0,
        ),
    )(lag_days, me, weights, *got)


def swap(sends, axis):
    count = lax.axis_size(axis)
    return [sends[0]] + [
        lax.ppermute(sends[hop], axis, [(i, peer(i, hop, count)[0]) for i in range(count)])
        for hop in range(1, count)
    ]


def gather(block, axis):
    count = lax.axis_size(axis)
    if count & (count - 1):
        return lax.all_gather(block, axis)
    me = lax.axis_index(axis)
    held = block[None]
    reach = 1
    while reach < count:
        other = lax.ppermute(held, axis, [(i, i ^ reach) for i in range(count)])
        upper = (me & reach) != 0
        held = jnp.concatenate(
            [jnp.where(upper, other, held), jnp.where(upper, held, other)], axis=0
        )
        reach *= 2
    return held


def plan_of(slot_local, days_local, day_block):
    pairs, blocks = slot_local // 2, days_local // day_block
    every = (0, blocks)
    if slot_local % 48 == 0 and blocks > 1:
        cut = pairs * 2 // 3
        sent = [(0, 0, pairs, (0, 1)), (0, 0, pairs, (1, blocks)), (1, 0, cut, every), (1, cut, pairs, every)]
        return sent, [(0, 1), (2,), (3,)]
    return [(0, 0, pairs, every), (1, 0, pairs, every)], [(0,), (1,)]


def body(daily_fields, order_table, lag_days, lag_weights):
    wide_count = lax.axis_size("wide")
    narrow_count = lax.axis_size("narrow")
    days_local, lat_local, lon_count = daily_fields.shape
    order_count = order_table.shape[0]
    slot_local = order_count // wide_count
    pair_local = slot_local // 2
    deg_local = lag_weights.shape[1]
    deg_count = deg_local * narrow_count
    kept_days = days_local * narrow_count - LAGMAX
    day_block = math.gcd(128 // math.gcd(128, lat_local), days_local)
    me = lax.axis_index("narrow").astype(jnp.int32).reshape(1)

    fields = daily_fields.reshape(days_local * lat_local, lon_count)
    parts = [jnp.asarray(p) for p in dft_columns(order_count, lon_count)]
    lat_table = jnp.asarray(lat_columns(deg_count, lat_local * wide_count))
    order_row = order_table.reshape(1, order_count)

    own_weights = jnp.transpose(
        lag_weights.reshape(3, deg_local, pair_local, 2, 2), (4, 3, 0, 2, 1)
    )
    all_weights = gather(own_weights, "narrow")
    all_weights = jnp.moveaxis(all_weights, 0, 4).reshape(2, 2, 3, pair_local, deg_count)

    def rows_of(weights, part, first, last):
        return jnp.concatenate([weights[part, parity, :, first:last] for parity in range(2)], axis=1)

    sent, jobs = plan_of(slot_local, days_local, day_block)
    spreads = {}
    picked = {}

    def product(index, after):
        part, first, last, blocks = sent[index]
        owned = (slot_local, first, last)
        return spectra_of(order_row, owned, parts[part], fields, day_block * lat_local, blocks, after)

    def exchange(spectra):
        spectra = spectra.reshape(wide_count, -1, spectra.shape[1])
        return lax.all_to_all(spectra, "wide", split_axis=0, concat_axis=0, tiled=True)

    def finish(job, after):
        part, first, last, _ = sent[job[0]]
        *sends, picks = digest(
            lag_days,
            me,
            [received[index] for index in job],
            lat_table,
            rows_of(all_weights, part, first, last),
            narrow_count,
            after,
        )
        total = combine(
            lag_days, me, rows_of(own_weights, part, first, last), swap(sends, "narrow")
        )
        for parity in range(2):
            rows = slice(parity * (last - first), (parity + 1) * (last - first))
            spreads[part, parity, first] = total[rows]
            if part == 0:
                picked[parity, first] = picks[:, rows]
        return total

    def panel_of():
        series = jnp.stack(
            [
                jnp.concatenate([picked[k] for k in sorted(picked) if k[0] == parity], axis=1)
                for parity in range(2)
            ],
            axis=2,
        )
        series = series.reshape(days_local, slot_local, narrow_count * (ROW_DEG + 1))
        series = jnp.transpose(series, (1, 2, 0)).reshape(slot_local, -1)
        series = gather(series, "narrow")
        series = series.reshape(narrow_count, slot_local, narrow_count, ROW_DEG + 1, days_local)
        series = jnp.moveaxis(series, 0, 3).reshape(
            slot_local, narrow_count, ROW_DEG + 1, days_local * narrow_count
        )
        weights = all_weights[0].reshape(2, 3, pair_local, narrow_count, deg_local)
        weights = jnp.transpose(weights[..., : ROW_DEG + 1], (1, 2, 0, 3, 4)).reshape(
            3, slot_local, narrow_count, ROW_DEG + 1, 1
        )
        residual = series[..., LAGMAX:].astype(jnp.float32)
        for position in range(3):
            shifted = lax.dynamic_slice_in_dim(series, LAGMAX - lag_days[position], kept_days, axis=3)
            residual = residual - weights[position] * shifted.astype(jnp.float32)
        rounded = residual.astype(jnp.bfloat16)
        rows = rounded[:, :, :ROW_DEG].reshape(slot_local, narrow_count * ROW_DEG, kept_days)
        column = lax.dynamic_index_in_dim(rounded[:, :, ROW_DEG], me[0], 1, False)
        columns = gather(column, "wide").reshape(order_count, kept_days)
        product = lax.dot_general(
            rows, columns, (((2,), (1,)), ((), ())), preferred_element_type=jnp.float32
        )
        return product / math.sqrt(kept_days)

    spectra = {0: product(0, [])}
    spectra[1] = before = product(1, [spectra[0]])
    for index in reversed(range(2, len(sent))):
        before = spectra[index] = product(index, [before, all_weights])
    received = [exchange(spectra[index]) for index in range(len(sent) - 1)]
    if len(sent) == 2:
        received.append(exchange(spectra[1]))
    done = [finish(jobs[0], [])]
    panel = panel_of()
    done.append(panel)
    if len(sent) > 2:
        received.append(exchange(tie(spectra[len(sent) - 1], done)))
    for job in jobs[1:]:
        done = [finish(job, done)]

    spread = jnp.stack(
        [
            jnp.stack(
                [
                    jnp.concatenate(
                        [spreads[k] for k in sorted(spreads) if k[:2] == (part, parity)], axis=0
                    )
                    for part in range(2)
                ]
            )
            for parity in range(2)
        ]
    )
    noise_variance = jnp.transpose(spread / kept_days, (3, 2, 0, 1)).reshape(deg_local, slot_local, 2)
    return (noise_variance, panel)


def solution(mesh):
    placed = (P("narrow", "wide", None), P(), P(), P(None, "narrow", "wide", None))
    return jax.shard_map(
        body,
        mesh=mesh,
        in_specs=placed,
        out_specs=(P("narrow", "wide", None), P("wide", None, "narrow")),
        check_vma=False,
    )
```

```python
import functools
import math

import jax
import jax.numpy as jnp
import numpy as np
from jax import lax
from jax.experimental import pallas as pl
from jax.experimental.pallas import tpu as pltpu
from jax.sharding import PartitionSpec as P

LAGMAX = 8
ROW_DEG = 3
VMEM = 40 * 2**20
FULL_VMEM = 63 * 2**20


def dft_columns(orders, longitudes):
    turns = np.arange(longitudes)[:, None] * np.arange(orders)[None, :] % longitudes
    angle = turns * (2.0 * np.pi / longitudes)
    scale = 1.0 / math.sqrt(longitudes)
    return np.stack([np.cos(angle) * scale, -np.sin(angle) * scale]).astype(jnp.bfloat16)


def lat_columns(degrees, latitudes):
    degree = np.arange(degrees)[None, :]
    odd_lat = 2 * np.arange(latitudes)[:, None] + 1
    period = 4 * latitudes
    unit = np.pi / (2 * latitudes)
    scale = math.sqrt(2.0 / latitudes)
    cosines = np.cos(degree * odd_lat % period * unit) * scale
    sines = np.sin((degree + 1) * odd_lat % period * unit) * scale
    return np.concatenate([cosines, sines], axis=1).astype(jnp.bfloat16)


ANY = pl.BlockSpec(memory_space=pl.ANY)
IN_HBM = pl.BlockSpec(memory_space=pltpu.HBM)
IN_VMEM = pl.BlockSpec(memory_space=pltpu.VMEM)
IN_SMEM = pl.BlockSpec(memory_space=pltpu.SMEM)


def picks_of(owned, order_ref):
    slot_local, first, last = owned
    slots = order_ref.shape[0]
    held = last - first
    rows = slots // slot_local * 2 * held
    column = lax.broadcasted_iota(jnp.int32, (1, rows), 1)
    owner, place = lax.div(column, 2 * held), lax.rem(column, 2 * held)
    odd = (place >= held).astype(jnp.int32)
    slot = owner * slot_local + 2 * (first + place - held * odd) + odd
    here = lax.broadcasted_iota(jnp.int32, (slots, rows), 0)
    orders = jnp.broadcast_to(order_ref[...].astype(jnp.float32).reshape(1, slots), (8, slots))
    chosen = jnp.dot(
        orders,
        (here == slot).astype(jnp.float32),
        precision=lax.Precision.HIGHEST,
        preferred_element_type=jnp.float32,
    )
    return (here.astype(jnp.float32) == chosen[:1]).astype(jnp.bfloat16)


def spectra_kernel(owned, order_ref, part_ref, field_ref, *refs):
    out_ref, table_ref = refs[-2:]

    @pl.when(pl.program_id(0) == 0)
    def _():
        table_ref[...] = jnp.dot(
            part_ref[...], picks_of(owned, order_ref), preferred_element_type=jnp.float32
        ).astype(jnp.bfloat16)

    cells = jnp.dot(field_ref[...], table_ref[...], preferred_element_type=jnp.float32)
    out_ref[...] = cells.T.astype(jnp.bfloat16)


def first_spectra_kernel(owned, part, order_ref, part_hbm, field_hbm, out_ref, part_ref, field_ref, sems):
    block = out_ref.shape[1]
    tiles = block // 128
    cuts = [128 * (tiles * i // 3) for i in range(4)]
    part_copy = pltpu.make_async_copy(part_hbm.at[part], part_ref, sems.at[0])
    copies = []
    for index in range(3):
        rows = pl.ds(cuts[index], cuts[index + 1] - cuts[index])
        copies.append(
            pltpu.make_async_copy(field_hbm.at[rows], field_ref.at[rows], sems.at[index + 1])
        )
    part_copy.start()
    copies[0].start()
    picks = picks_of(owned, order_ref)
    part_copy.wait()
    for copy in copies[1:]:
        copy.start()
    table = jnp.dot(part_ref[...], picks, preferred_element_type=jnp.float32).astype(jnp.bfloat16)
    for start, stop, copy in zip(cuts, cuts[1:], copies):
        copy.wait()
        cells = jnp.dot(field_ref[start:stop], table, preferred_element_type=jnp.float32)
        out_ref[:, start:stop] = cells.T.astype(jnp.bfloat16)


def spectra_of(order_table, owned, parts, part, fields, block, blocks, after):
    lon_count = fields.shape[1]
    first, last = blocks
    slot_local, first_pair, last_pair = owned
    rows = order_table.shape[0] // slot_local * 2 * (last_pair - first_pair)
    cells = (last - first) * block
    alone = blocks == (0, 1) and block % 128 == 0 and block > 256 and not after
    cost = pl.CostEstimate(
        flops=2 * rows * cells * lon_count,
        bytes_accessed=2 * (cells * lon_count + rows * (cells + lon_count)),
        transcendentals=0,
    )
    out_shape = jax.ShapeDtypeStruct((rows, cells), jnp.bfloat16)
    params = pltpu.CompilerParams(vmem_limit_bytes=FULL_VMEM)
    if alone:
        return pl.pallas_call(
            functools.partial(first_spectra_kernel, owned, part),
            in_specs=[IN_VMEM, IN_HBM, IN_HBM],
            out_specs=IN_VMEM,
            out_shape=out_shape,
            scratch_shapes=[
                pltpu.VMEM(parts.shape[1:], jnp.bfloat16),
                pltpu.VMEM((block, lon_count), jnp.bfloat16),
                pltpu.SemaphoreType.DMA((4,)),
            ],
            compiler_params=params,
            cost_estimate=cost,
        )(order_table, parts, fields)
    return pl.pallas_call(
        functools.partial(spectra_kernel, owned),
        grid=(last - first,),
        in_specs=[
            pl.BlockSpec(order_table.shape, lambda i: (0,)),
            pl.BlockSpec((None,) + parts.shape[1:], lambda i: (part, 0, 0)),
            pl.BlockSpec((block, lon_count), lambda i: (i + first, 0)),
        ]
        + [ANY] * len(after),
        out_specs=pl.BlockSpec((rows, block), lambda i: (0, i)),
        out_shape=out_shape,
        scratch_shapes=[pltpu.VMEM((lon_count, rows), jnp.bfloat16)],
        compiler_params=params,
        cost_estimate=cost,
    )(order_table, parts, fields, *after)


def peer(me, hop, count):
    if count & (count - 1) == 0:
        return me ^ hop, me ^ hop
    return (me + hop) % count, (me - hop + count) % count


def digest_kernel(shape, lag_ref, me_ref, weight_ref, lat_hbm, *refs):
    groups, narrow_count, lat_local, n_after = shape
    blocks, refs = refs[:groups], refs[groups + n_after :]
    lat_ref, lat_sem = refs[-2:]
    refs = refs[:-2]
    lat_copy = pltpu.make_async_copy(lat_hbm, lat_ref, lat_sem)
    lat_copy.start()
    sends, pick_refs = refs[:narrow_count], refs[narrow_count:-3]
    line_ref, series_ref, block_ref = refs[-3:]
    days, slots, degrees = series_ref.shape
    half, padded = slots // 2, line_ref.shape[1] // 2
    start = 0
    for block in blocks:
        stop = start + block.shape[2] // lat_local
        for day in range(start, stop):
            cells = slice((day - start) * lat_local, (day - start + 1) * lat_local)
            for source in range(block.shape[0]):
                lats = slice(source * lat_local, (source + 1) * lat_local)
                if half == padded:
                    line_ref[day, :, lats] = block[source, :, cells]
                else:
                    line_ref[day, :half, lats] = block[source, :half, cells]
                    line_ref[day, padded : padded + half, lats] = block[source, half:, cells]
        if start == 0:
            lat_copy.wait()
        for parity in range(2):
            lines = line_ref[start:stop, parity * padded : (parity + 1) * padded, :]
            coeffs = jnp.dot(
                lines.reshape((stop - start) * padded, lat_ref.shape[0]),
                lat_ref[:, parity * degrees : (parity + 1) * degrees],
                preferred_element_type=jnp.float32,
            )
            coeffs = coeffs.astype(jnp.bfloat16).reshape(stop - start, padded, degrees)
            series_ref[start:stop, parity * half : (parity + 1) * half, :] = coeffs[:, :half]
        start = stop

    step = 16 if slots % 16 == 0 else slots
    lags = [lag_ref[i] for i in range(3)]
    deg_local = degrees // narrow_count
    for first in range(0, slots, step):
        rows = pl.ds(first, step)
        weights = [weight_ref[i, rows, :] for i in range(3)]

        def add_day(day, total):
            residual = series_ref[day, rows, :].astype(jnp.float32)
            for lag, weight in zip(lags, weights):
                residual = residual - weight * series_ref[day - lag, rows, :].astype(jnp.float32)
            return total + residual * residual

        total = lax.fori_loop(
            LAGMAX, days, add_day, jnp.zeros((step, degrees), jnp.float32), unroll=4
        )
        coarse = total.astype(jnp.bfloat16)
        fine = (total - coarse.astype(jnp.float32)).astype(jnp.bfloat16)
        for owner in range(narrow_count):
            own = slice(owner * deg_local, (owner + 1) * deg_local)
            block_ref[owner, :LAGMAX, rows, :] = series_ref[:LAGMAX, rows, own]
            block_ref[owner, LAGMAX : 2 * LAGMAX, rows, :] = series_ref[days - LAGMAX :, rows, own]
            block_ref[owner, 2 * LAGMAX, rows, :] = coarse[:, own]
            block_ref[owner, 2 * LAGMAX + 1, rows, :] = fine[:, own]
    for pick_ref in pick_refs:
        for owner in range(narrow_count):
            kept = slice(owner * (ROW_DEG + 1), (owner + 1) * (ROW_DEG + 1))
            first = owner * deg_local
            pick_ref[:, :, kept] = series_ref[:, :, first : first + ROW_DEG + 1]
    me = me_ref[0]
    for hop, send in enumerate(sends):
        send[...] = block_ref[peer(me, hop, narrow_count)[0]]


def digest(lag_days, me, received, lat_table, weights, narrow_count, wants_picks, after):
    sources, slots, _ = received[0].shape
    latitudes, degrees = lat_table.shape[0], lat_table.shape[1] // 2
    lat_local = latitudes // sources
    days_local = sum(block.shape[2] for block in received) // lat_local
    deg_local = degrees // narrow_count
    padded = 2 * (-(-(slots // 2) // 8) * 8)
    message = (2 * LAGMAX + 2, slots, deg_local)
    picked = (days_local, slots, narrow_count * (ROW_DEG + 1))
    return pl.pallas_call(
        functools.partial(digest_kernel, (len(received), narrow_count, lat_local, len(after))),
        in_specs=[IN_SMEM, IN_SMEM, IN_VMEM, IN_HBM] + [IN_VMEM] * len(received) + [ANY] * len(after),
        out_specs=[IN_VMEM] * (narrow_count + wants_picks),
        out_shape=[jax.ShapeDtypeStruct(message, jnp.bfloat16)] * narrow_count
        + [jax.ShapeDtypeStruct(picked, jnp.bfloat16)] * wants_picks,
        scratch_shapes=[
            pltpu.VMEM((days_local, padded, latitudes), jnp.bfloat16),
            pltpu.VMEM((days_local, slots, degrees), jnp.bfloat16),
            pltpu.VMEM((narrow_count,) + message, jnp.bfloat16),
            pltpu.VMEM(lat_table.shape, jnp.bfloat16),
            pltpu.SemaphoreType.DMA(()),
        ],
        compiler_params=pltpu.CompilerParams(vmem_limit_bytes=VMEM if slots > 32 else VMEM // 2),
        cost_estimate=pl.CostEstimate(
            flops=4 * slots * days_local * latitudes * degrees,
            bytes_accessed=2 * slots * days_local * (latitudes + degrees),
            transcendentals=0,
        ),
    )(lag_days, me, weights, lat_table, *received, *after)


def tie(array, after):
    return pl.pallas_call(
        lambda *refs: None,
        in_specs=[ANY] * (1 + len(after)),
        out_specs=ANY,
        out_shape=jax.ShapeDtypeStruct(array.shape, array.dtype),
        input_output_aliases={0: 0},
    )(array, *after)


def combine_kernel(count, lag_ref, me_ref, weight_ref, *refs):
    got, out_ref, seam_ref, sum_ref = refs[:count], refs[count], refs[count + 1], refs[count + 2]
    me = me_ref[0]
    total = jnp.zeros(out_ref.shape, jnp.float32)
    for hop in range(count):
        source = peer(me, hop, count)[1]
        seam_ref[source, LAGMAX:] = got[hop][:LAGMAX]
        seam_ref[source + 1, :LAGMAX] = got[hop][LAGMAX : 2 * LAGMAX]
        sums = got[hop][2 * LAGMAX :].astype(jnp.float32)
        sum_ref[source] = sums[0] + sums[1]
    for source in range(count):
        total = total + sum_ref[source]
    lags = [lag_ref[i] for i in range(3)]
    weights = [weight_ref[i] for i in range(3)]
    for block in range(1, count):
        for day in range(LAGMAX, 2 * LAGMAX):
            residual = seam_ref[block, day].astype(jnp.float32)
            for lag, weight in zip(lags, weights):
                residual = residual - weight * seam_ref[block, day - lag].astype(jnp.float32)
            total = total + residual * residual
    out_ref[...] = total


def combine(lag_days, me, weights, got):
    count = len(got)
    days, slots, degrees = got[0].shape
    return pl.pallas_call(
        functools.partial(combine_kernel, count),
        in_specs=[IN_SMEM, IN_SMEM] + [IN_VMEM] * (count + 1),
        out_specs=IN_VMEM,
        out_shape=jax.ShapeDtypeStruct((slots, degrees), jnp.float32),
        scratch_shapes=[
            pltpu.VMEM((count + 1, 2 * LAGMAX, slots, degrees), jnp.bfloat16),
            pltpu.VMEM((count, slots, degrees), jnp.float32),
        ],
        compiler_params=pltpu.CompilerParams(vmem_limit_bytes=VMEM // 2),
        cost_estimate=pl.CostEstimate(
            flops=8 * count * LAGMAX * slots * degrees,
            bytes_accessed=2 * count * days * slots * degrees,
            transcendentals=0,
        ),
    )(lag_days, me, weights, *got)


def swap(sends, axis):
    count = lax.axis_size(axis)
    return [sends[0]] + [
        lax.ppermute(sends[hop], axis, [(i, peer(i, hop, count)[0]) for i in range(count)])
        for hop in range(1, count)
    ]


def gather_step(held, depth, axis):
    count = lax.axis_size(axis)
    reach = count >> (depth + 1)
    other = lax.ppermute(held, axis, [(i, i ^ reach) for i in range(count)])
    upper = (lax.axis_index(axis) & reach) != 0
    return jnp.stack([jnp.where(upper, other, held), jnp.where(upper, held, other)], axis=depth)


def gather(block, axis, held=None):
    count = lax.axis_size(axis)
    if count & (count - 1):
        return lax.all_gather(block, axis)
    depth = 0 if held is None else 1
    held = block if held is None else held
    while count >> (depth + 1):
        held, depth = gather_step(held, depth, axis), depth + 1
    return held.reshape((count,) + block.shape)


def plan_of(slot_local, days_local, day_block):
    pairs, blocks = slot_local // 2, days_local // day_block
    every = (0, blocks)
    if slot_local % 48 == 0 and blocks > 1:
        cut = pairs * 2 // 3
        sent = [(0, 0, pairs, (0, 1)), (0, 0, pairs, (1, blocks)), (1, 0, cut, every), (1, cut, pairs, every)]
        return sent, [(0, 1), (2,), (3,)]
    return [(0, 0, pairs, every), (1, 0, pairs, every)], [(0,), (1,)]


def body(daily_fields, order_table, lag_days, lag_weights):
    wide_count = lax.axis_size("wide")
    narrow_count = lax.axis_size("narrow")
    days_local, lat_local, lon_count = daily_fields.shape
    order_count = order_table.shape[0]
    slot_local = order_count // wide_count
    pair_local = slot_local // 2
    deg_local = lag_weights.shape[1]
    deg_count = deg_local * narrow_count
    kept_days = days_local * narrow_count - LAGMAX
    day_block = math.gcd(128 // math.gcd(128, lat_local), days_local)
    me = lax.axis_index("narrow").astype(jnp.int32).reshape(1)

    fields = daily_fields.reshape(days_local * lat_local, lon_count)
    parts = jnp.asarray(dft_columns(order_count, lon_count))
    lat_table = jnp.asarray(lat_columns(deg_count, lat_local * wide_count))
    own_weights = jnp.transpose(
        lag_weights.reshape(3, deg_local, pair_local, 2, 2), (4, 3, 0, 2, 1)
    )
    all_weights = gather(own_weights, "narrow")
    all_weights = jnp.moveaxis(all_weights, 0, 4).reshape(2, 2, 3, pair_local, deg_count)

    def rows_of(weights, part, first, last):
        return jnp.concatenate([weights[part, parity, :, first:last] for parity in range(2)], axis=1)

    sent, jobs = plan_of(slot_local, days_local, day_block)
    spreads = {}
    picked = {}

    def product(index, after):
        part, first, last, blocks = sent[index]
        owned = (slot_local, first, last)
        return spectra_of(order_table, owned, parts, part, fields, day_block * lat_local, blocks, after)

    def exchange(spectra):
        spectra = spectra.reshape(wide_count, -1, spectra.shape[1])
        return lax.all_to_all(spectra, "wide", split_axis=0, concat_axis=0, tiled=True)

    def finish(job, after):
        part, first, last, _ = sent[job[0]]
        out = digest(
            lag_days,
            me,
            [received[index] for index in job],
            lat_table,
            rows_of(all_weights, part, first, last),
            narrow_count,
            part == 0,
            after,
        )
        sends, picks = out[:narrow_count], out[narrow_count:]
        total = combine(
            lag_days, me, rows_of(own_weights, part, first, last), swap(sends, "narrow")
        )
        for parity in range(2):
            rows = slice(parity * (last - first), (parity + 1) * (last - first))
            spreads[part, parity, first] = total[rows]
            if picks:
                picked[parity, first] = picks[0][:, rows]
        return total

    def panel_rows():
        series = jnp.stack(
            [
                jnp.concatenate([picked[k] for k in sorted(picked) if k[0] == parity], axis=1)
                for parity in range(2)
            ],
            axis=2,
        )
        series = series.reshape(days_local, slot_local, narrow_count * (ROW_DEG + 1))
        series = jnp.transpose(series, (1, 2, 0)).reshape(slot_local, -1)
        series = gather(series, "narrow")
        series = series.reshape(narrow_count, slot_local, narrow_count, ROW_DEG + 1, days_local)
        series = jnp.moveaxis(series, 0, 3).reshape(
            slot_local, narrow_count, ROW_DEG + 1, days_local * narrow_count
        )
        weights = all_weights[0].reshape(2, 3, pair_local, narrow_count, deg_local)
        weights = jnp.transpose(weights[..., : ROW_DEG + 1], (1, 2, 0, 3, 4)).reshape(
            3, slot_local, narrow_count, ROW_DEG + 1, 1
        )
        residual = series[..., LAGMAX:].astype(jnp.float32)
        for position in range(3):
            shifted = lax.dynamic_slice_in_dim(series, LAGMAX - lag_days[position], kept_days, axis=3)
            residual = residual - weights[position] * shifted.astype(jnp.float32)
        rounded = residual.astype(jnp.bfloat16)
        rows = rounded[:, :, :ROW_DEG].reshape(slot_local, narrow_count * ROW_DEG, kept_days)
        column = lax.dynamic_index_in_dim(rounded[:, :, ROW_DEG], me[0], 1, False)
        held = column if wide_count & (wide_count - 1) else gather_step(column, 0, "wide")
        return rows, column, held

    def panel_of(rows, column, held):
        columns = gather(column, "wide", held).reshape(order_count, kept_days)
        product = lax.dot_general(
            rows, columns, (((2,), (1,)), ((), ())), preferred_element_type=jnp.float32
        )
        return product / math.sqrt(kept_days)

    spectra = {0: product(0, [])}
    spectra[1] = before = product(1, [spectra[0]])
    for index in reversed(range(2, len(sent))):
        before = spectra[index] = product(index, [before, all_weights])
    received = [exchange(spectra[index]) for index in range(len(sent) - 1)]
    if len(sent) == 2:
        received.append(exchange(spectra[1]))
    done = [finish(jobs[0], [])]
    rows, column, held = panel_rows()
    if len(sent) > 2:
        received.append(exchange(tie(spectra[len(sent) - 1], done + [held])))
    panel = panel_of(rows, column, held)
    for job in jobs[1:-1]:
        done.append(finish(job, []))
    finish(jobs[-1], done + [panel])

    spread = jnp.stack(
        [
            jnp.stack(
                [
                    jnp.concatenate(
                        [spreads[k] for k in sorted(spreads) if k[:2] == (part, parity)], axis=0
                    )
                    for part in range(2)
                ]
            )
            for parity in range(2)
        ]
    )
    noise_variance = jnp.transpose(spread / kept_days, (3, 2, 0, 1)).reshape(deg_local, slot_local, 2)
    return (noise_variance, panel)


def solution(mesh):
    placed = (P("narrow", "wide", None), P(), P(), P(None, "narrow", "wide", None))
    return jax.shard_map(
        body,
        mesh=mesh,
        in_specs=placed,
        out_specs=(P("narrow", "wide", None), P("wide", None, "narrow")),
        check_vma=False,
    )
```

```python
import functools
import math

import jax
import jax.numpy as jnp
import numpy as np
from jax import lax
from jax.experimental import pallas as pl
from jax.experimental.pallas import tpu as pltpu
from jax.sharding import PartitionSpec as P

LAGMAX = 8
ROW_DEG = 3
VMEM = 40 * 2**20
FULL_VMEM = 63 * 2**20


def dft_columns(orders, longitudes):
    turns = np.arange(longitudes)[:, None] * np.arange(orders)[None, :] % longitudes
    angle = turns * (2.0 * np.pi / longitudes)
    scale = 1.0 / math.sqrt(longitudes)
    return np.stack([np.cos(angle) * scale, -np.sin(angle) * scale]).astype(jnp.bfloat16)


def lat_columns(degrees, latitudes):
    degree = np.arange(degrees)[None, :]
    odd_lat = 2 * np.arange(latitudes)[:, None] + 1
    period = 4 * latitudes
    unit = np.pi / (2 * latitudes)
    scale = math.sqrt(2.0 / latitudes)
    cosines = np.cos(degree * odd_lat % period * unit) * scale
    sines = np.sin((degree + 1) * odd_lat % period * unit) * scale
    return np.concatenate([cosines, sines], axis=1).astype(jnp.bfloat16)


ANY = pl.BlockSpec(memory_space=pl.ANY)
IN_HBM = pl.BlockSpec(memory_space=pltpu.HBM)
IN_VMEM = pl.BlockSpec(memory_space=pltpu.VMEM)
IN_SMEM = pl.BlockSpec(memory_space=pltpu.SMEM)


def picks_of(owned, order_ref, swapped=0):
    slot_local, first, last = owned
    slots = order_ref.shape[0]
    held = last - first
    rows = slots // slot_local * 2 * held
    column = lax.broadcasted_iota(jnp.int32, (1, rows), 1)
    owner, place = lax.div(column, 2 * held) ^ swapped, lax.rem(column, 2 * held)
    odd = (place >= held).astype(jnp.int32)
    slot = owner * slot_local + 2 * (first + place - held * odd) + odd
    here = lax.broadcasted_iota(jnp.int32, (slots, rows), 0)
    orders = jnp.broadcast_to(order_ref[...].astype(jnp.float32).reshape(1, slots), (8, slots))
    chosen = jnp.dot(
        orders,
        (here == slot).astype(jnp.float32),
        precision=lax.Precision.HIGHEST,
        preferred_element_type=jnp.float32,
    )
    return (here.astype(jnp.float32) == chosen[:1]).astype(jnp.bfloat16)


def spectra_kernel(owned, order_ref, part_ref, field_ref, *refs):
    out_ref, table_ref = refs[-2:]

    @pl.when(pl.program_id(0) == 0)
    def _():
        table_ref[...] = jnp.dot(
            part_ref[...], picks_of(owned, order_ref), preferred_element_type=jnp.float32
        ).astype(jnp.bfloat16)

    cells = jnp.dot(field_ref[...], table_ref[...], preferred_element_type=jnp.float32)
    out_ref[...] = cells.T.astype(jnp.bfloat16)


def first_spectra_kernel(owned, part, order_ref, part_hbm, field_hbm, *refs):
    outs, (part_ref, field_ref, sems) = refs[:-3], refs[-3:]
    rows, block = outs[0].shape
    tiles = block // 128
    cuts = [128 * (tiles * i // 3) for i in range(4)]
    part_copy = pltpu.make_async_copy(part_hbm.at[part], part_ref, sems.at[0])
    copies = []
    for index in range(3):
        cells = pl.ds(cuts[index], cuts[index + 1] - cuts[index])
        copies.append(
            pltpu.make_async_copy(field_hbm.at[cells], field_ref.at[cells], sems.at[index + 1])
        )
    part_copy.start()
    copies[0].start()
    picks = picks_of(owned, order_ref, lax.axis_index("wide"))
    part_copy.wait()
    for copy in copies[1:]:
        copy.start()
    table = jnp.dot(part_ref[...], picks, preferred_element_type=jnp.float32).astype(jnp.bfloat16)
    for start, stop, copy in zip(cuts, cuts[1:], copies):
        copy.wait()
        cells = jnp.dot(field_ref[start:stop], table, preferred_element_type=jnp.float32)
        cells = cells.T.astype(jnp.bfloat16)
        for hop, out_ref in enumerate(outs):
            out_ref[:, start:stop] = cells[hop * rows : (hop + 1) * rows]


def first_spectra_of(order_table, owned, parts, part, fields, block):
    lon_count = fields.shape[1]
    slot_local, first_pair, last_pair = owned
    hops = order_table.shape[0] // slot_local
    rows = 2 * (last_pair - first_pair)
    return pl.pallas_call(
        functools.partial(first_spectra_kernel, owned, part),
        in_specs=[IN_VMEM, IN_HBM, IN_HBM],
        out_specs=[IN_VMEM] * hops,
        out_shape=[jax.ShapeDtypeStruct((rows, block), jnp.bfloat16)] * hops,
        scratch_shapes=[
            pltpu.VMEM(parts.shape[1:], jnp.bfloat16),
            pltpu.VMEM((block, lon_count), jnp.bfloat16),
            pltpu.SemaphoreType.DMA((4,)),
        ],
        compiler_params=pltpu.CompilerParams(vmem_limit_bytes=FULL_VMEM),
        cost_estimate=pl.CostEstimate(
            flops=2 * hops * rows * block * lon_count,
            bytes_accessed=2 * (block * lon_count + hops * rows * (block + lon_count)),
            transcendentals=0,
        ),
    )(order_table, parts, fields)


def spectra_of(order_table, owned, parts, part, fields, block, blocks, after):
    lon_count = fields.shape[1]
    first, last = blocks
    slot_local, first_pair, last_pair = owned
    rows = order_table.shape[0] // slot_local * 2 * (last_pair - first_pair)
    cells = (last - first) * block
    cost = pl.CostEstimate(
        flops=2 * rows * cells * lon_count,
        bytes_accessed=2 * (cells * lon_count + rows * (cells + lon_count)),
        transcendentals=0,
    )
    out_shape = jax.ShapeDtypeStruct((rows, cells), jnp.bfloat16)
    params = pltpu.CompilerParams(vmem_limit_bytes=FULL_VMEM)
    return pl.pallas_call(
        functools.partial(spectra_kernel, owned),
        grid=(last - first,),
        in_specs=[
            pl.BlockSpec(order_table.shape, lambda i: (0,)),
            pl.BlockSpec((None,) + parts.shape[1:], lambda i: (part, 0, 0)),
            pl.BlockSpec((block, lon_count), lambda i: (i + first, 0)),
        ]
        + [ANY] * len(after),
        out_specs=pl.BlockSpec((rows, block), lambda i: (0, i)),
        out_shape=out_shape,
        scratch_shapes=[pltpu.VMEM((lon_count, rows), jnp.bfloat16)],
        compiler_params=params,
        cost_estimate=cost,
    )(order_table, parts, fields, *after)


def peer(me, hop, count):
    if count & (count - 1) == 0:
        return me ^ hop, me ^ hop
    return (me + hop) % count, (me - hop + count) % count


def digest_kernel(shape, lag_ref, me_ref, weight_ref, lat_hbm, *refs):
    groups, hops, narrow_count, lat_local, n_after = shape
    by_hop, blocks, refs = refs[:hops], list(refs[hops : hops + groups]), refs[hops + groups + n_after :]
    lat_ref, stage_ref, sems = refs[-3:]
    refs = refs[:-3]
    copies = [pltpu.make_async_copy(lat_hbm, lat_ref, sems.at[hops])]
    for hop, ref in enumerate(by_hop):
        source = me_ref[1] ^ hop
        copies.append(pltpu.make_async_copy(ref, stage_ref.at[source], sems.at[hop]))
    for copy in copies:
        copy.start()
    if hops:
        blocks.insert(0, stage_ref)
        for copy in copies[1:]:
            copy.wait()
    sends, pick_refs = refs[:narrow_count], refs[narrow_count:-3]
    line_ref, series_ref, block_ref = refs[-3:]
    days, slots, degrees = series_ref.shape
    half, padded = slots // 2, line_ref.shape[1] // 2
    start = 0
    for block in blocks:
        stop = start + block.shape[2] // lat_local
        for day in range(start, stop):
            cells = slice((day - start) * lat_local, (day - start + 1) * lat_local)
            for source in range(block.shape[0]):
                lats = slice(source * lat_local, (source + 1) * lat_local)
                if half == padded:
                    line_ref[day, :, lats] = block[source, :, cells]
                else:
                    line_ref[day, :half, lats] = block[source, :half, cells]
                    line_ref[day, padded : padded + half, lats] = block[source, half:, cells]
        if start == 0:
            copies[0].wait()
        for parity in range(2):
            lines = line_ref[start:stop, parity * padded : (parity + 1) * padded, :]
            coeffs = jnp.dot(
                lines.reshape((stop - start) * padded, lat_ref.shape[0]),
                lat_ref[:, parity * degrees : (parity + 1) * degrees],
                preferred_element_type=jnp.float32,
            )
            coeffs = coeffs.astype(jnp.bfloat16).reshape(stop - start, padded, degrees)
            series_ref[start:stop, parity * half : (parity + 1) * half, :] = coeffs[:, :half]
        start = stop

    step = 16 if slots % 16 == 0 else slots
    lags = [lag_ref[i] for i in range(3)]
    deg_local = degrees // narrow_count
    for first in range(0, slots, step):
        rows = pl.ds(first, step)
        weights = [weight_ref[i, rows, :] for i in range(3)]

        def add_day(day, total):
            residual = series_ref[day, rows, :].astype(jnp.float32)
            for lag, weight in zip(lags, weights):
                residual = residual - weight * series_ref[day - lag, rows, :].astype(jnp.float32)
            return total + residual * residual

        total = lax.fori_loop(
            LAGMAX, days, add_day, jnp.zeros((step, degrees), jnp.float32), unroll=4
        )
        coarse = total.astype(jnp.bfloat16)
        fine = (total - coarse.astype(jnp.float32)).astype(jnp.bfloat16)
        for owner in range(narrow_count):
            own = slice(owner * deg_local, (owner + 1) * deg_local)
            block_ref[owner, :LAGMAX, rows, :] = series_ref[:LAGMAX, rows, own]
            block_ref[owner, LAGMAX : 2 * LAGMAX, rows, :] = series_ref[days - LAGMAX :, rows, own]
            block_ref[owner, 2 * LAGMAX, rows, :] = coarse[:, own]
            block_ref[owner, 2 * LAGMAX + 1, rows, :] = fine[:, own]
    for pick_ref in pick_refs:
        for owner in range(narrow_count):
            kept = slice(owner * (ROW_DEG + 1), (owner + 1) * (ROW_DEG + 1))
            first = owner * deg_local
            pick_ref[:, :, kept] = series_ref[:, :, first : first + ROW_DEG + 1]
    me = me_ref[0]
    for hop, send in enumerate(sends):
        send[...] = block_ref[peer(me, hop, narrow_count)[0]]


def digest(lag_days, me, received, lat_table, weights, narrow_count, wants_picks, after):
    by_hop = received[0] if isinstance(received[0], list) else []
    received = received[1:] if by_hop else received
    sources, slots, _ = received[0].shape
    latitudes, degrees = lat_table.shape[0], lat_table.shape[1] // 2
    lat_local = latitudes // sources
    days_local = sum(block.shape[-1] for block in by_hop[:1] + received) // lat_local
    deg_local = degrees // narrow_count
    padded = 2 * (-(-(slots // 2) // 8) * 8)
    message = (2 * LAGMAX + 2, slots, deg_local)
    picked = (days_local, slots, narrow_count * (ROW_DEG + 1))
    return pl.pallas_call(
        functools.partial(
            digest_kernel, (len(received), len(by_hop), narrow_count, lat_local, len(after))
        ),
        in_specs=[IN_SMEM, IN_SMEM, IN_VMEM, IN_HBM]
        + [ANY] * len(by_hop)
        + [IN_VMEM] * len(received)
        + [ANY] * len(after),
        out_specs=[IN_VMEM] * (narrow_count + wants_picks),
        out_shape=[jax.ShapeDtypeStruct(message, jnp.bfloat16)] * narrow_count
        + [jax.ShapeDtypeStruct(picked, jnp.bfloat16)] * wants_picks,
        scratch_shapes=[
            pltpu.VMEM((days_local, padded, latitudes), jnp.bfloat16),
            pltpu.VMEM((days_local, slots, degrees), jnp.bfloat16),
            pltpu.VMEM((narrow_count,) + message, jnp.bfloat16),
            pltpu.VMEM(lat_table.shape, jnp.bfloat16),
            pltpu.VMEM((sources,) + by_hop[0].shape if by_hop else (8, 128), jnp.bfloat16),
            pltpu.SemaphoreType.DMA((len(by_hop) + 1,)),
        ],
        compiler_params=pltpu.CompilerParams(vmem_limit_bytes=VMEM if slots > 32 else VMEM // 2 if slots > 16 else FULL_VMEM - 2**20),
        cost_estimate=pl.CostEstimate(
            flops=4 * slots * days_local * latitudes * degrees,
            bytes_accessed=2 * slots * days_local * (latitudes + degrees),
            transcendentals=0,
        ),
    )(lag_days, me, weights, lat_table, *by_hop, *received, *after)


def tie(array, after):
    return pl.pallas_call(
        lambda *refs: None,
        in_specs=[ANY] * (1 + len(after)),
        out_specs=ANY,
        out_shape=jax.ShapeDtypeStruct(array.shape, array.dtype),
        input_output_aliases={0: 0},
    )(array, *after)


def combine_kernel(count, final, lag_ref, me_ref, weight_ref, *refs):
    got, others, (out_ref, seam_ref, sum_ref) = refs[:count], refs[count:-3], refs[-3:]
    me = me_ref[0]
    total = jnp.zeros(sum_ref.shape[1:], jnp.float32)
    for hop in range(count):
        source = peer(me, hop, count)[1]
        seam_ref[source, LAGMAX:] = got[hop][:LAGMAX]
        seam_ref[source + 1, :LAGMAX] = got[hop][LAGMAX : 2 * LAGMAX]
        sums = got[hop][2 * LAGMAX :].astype(jnp.float32)
        sum_ref[source] = sums[0] + sums[1]
    for source in range(count):
        total = total + sum_ref[source]
    lags = [lag_ref[i] for i in range(3)]
    weights = [weight_ref[i] for i in range(3)]
    for block in range(1, count):
        for day in range(LAGMAX, 2 * LAGMAX):
            residual = seam_ref[block, day].astype(jnp.float32)
            for lag, weight in zip(lags, weights):
                residual = residual - weight * seam_ref[block, day - lag].astype(jnp.float32)
            total = total + residual * residual
    if final is None:
        out_ref[...] = total
        return
    sum_ref[0] = total
    kept_days, places = final
    for source, (part, first, last) in zip([*others, sum_ref.at[0]], places):
        held = last - first
        for parity in range(2):
            for pair in range(first, last):
                row = parity * held + pair - first
                out_ref[2 * pair + parity, part : part + 1, :] = (
                    source[row : row + 1, :] / kept_days
                )


def combine(lag_days, me, weights, got, others=(), final=None):
    count = len(got)
    days, slots, degrees = got[0].shape
    shape = (slots, degrees)
    if final is not None:
        shape = (2 * max(last for _, _, last in final[1]), 2, degrees)
    return pl.pallas_call(
        functools.partial(combine_kernel, count, final),
        in_specs=[IN_SMEM, IN_SMEM] + [IN_VMEM] * (count + 1 + len(others)),
        out_specs=IN_VMEM,
        out_shape=jax.ShapeDtypeStruct(shape, jnp.float32),
        scratch_shapes=[
            pltpu.VMEM((count + 1, 2 * LAGMAX, slots, degrees), jnp.bfloat16),
            pltpu.VMEM((count, slots, degrees), jnp.float32),
        ],
        compiler_params=pltpu.CompilerParams(vmem_limit_bytes=VMEM // 2),
        cost_estimate=pl.CostEstimate(
            flops=8 * count * LAGMAX * slots * degrees,
            bytes_accessed=2 * count * days * slots * degrees,
            transcendentals=0,
        ),
    )(lag_days, me, weights, *got, *others)


def swap(sends, axis):
    count = lax.axis_size(axis)
    return [sends[0]] + [
        lax.ppermute(sends[hop], axis, [(i, peer(i, hop, count)[0]) for i in range(count)])
        for hop in range(1, count)
    ]


def gather_swap(held, depth, axis):
    count = lax.axis_size(axis)
    reach = count >> (depth + 1)
    return lax.ppermute(held, axis, [(i, i ^ reach) for i in range(count)])


def gather(block, axis, other=None):
    count = lax.axis_size(axis)
    if count & (count - 1):
        return lax.all_gather(block, axis)
    held, depth = block, 0
    while count >> (depth + 1):
        if depth or other is None:
            other = gather_swap(held, depth, axis)
        upper = (lax.axis_index(axis) & (count >> (depth + 1))) != 0
        pair = [jnp.where(upper, other, held), jnp.where(upper, held, other)]
        held, depth = jnp.stack(pair, axis=depth), depth + 1
    return held.reshape((count,) + block.shape)


def plan_of(slot_local, days_local, day_block, wide_count):
    pairs, blocks = slot_local // 2, days_local // day_block
    every = (0, blocks)
    if slot_local % 48 == 0 and blocks > 1 and wide_count & (wide_count - 1) == 0:
        cut = pairs * 2 // 3
        sent = [(0, 0, pairs, (0, 1)), (0, 0, pairs, (1, blocks)), (1, 0, cut, every), (1, cut, pairs, every)]
        return sent, [(0, 1), (2,), (3,)]
    return [(0, 0, pairs, every), (1, 0, pairs, every)], [(0,), (1,)]


def body(daily_fields, order_table, lag_days, lag_weights):
    wide_count = lax.axis_size("wide")
    narrow_count = lax.axis_size("narrow")
    days_local, lat_local, lon_count = daily_fields.shape
    order_count = order_table.shape[0]
    slot_local = order_count // wide_count
    pair_local = slot_local // 2
    deg_local = lag_weights.shape[1]
    deg_count = deg_local * narrow_count
    kept_days = days_local * narrow_count - LAGMAX
    day_block = math.gcd(128 // math.gcd(128, lat_local), days_local)
    me = jnp.stack([lax.axis_index("narrow"), lax.axis_index("wide")]).astype(jnp.int32)

    fields = daily_fields.reshape(days_local * lat_local, lon_count)
    parts = jnp.asarray(dft_columns(order_count, lon_count))
    lat_table = jnp.asarray(lat_columns(deg_count, lat_local * wide_count))
    own_weights = jnp.transpose(
        lag_weights.reshape(3, deg_local, pair_local, 2, 2), (4, 3, 0, 2, 1)
    )
    all_weights = gather(own_weights, "narrow")
    all_weights = jnp.moveaxis(all_weights, 0, 4).reshape(2, 2, 3, pair_local, deg_count)

    def rows_of(weights, part, first, last):
        return jnp.concatenate([weights[part, parity, :, first:last] for parity in range(2)], axis=1)

    sent, jobs = plan_of(slot_local, days_local, day_block, wide_count)
    picked = {}

    def product(index, after):
        part, first, last, blocks = sent[index]
        owned = (slot_local, first, last)
        return spectra_of(order_table, owned, parts, part, fields, day_block * lat_local, blocks, after)

    def first_exchange():
        part, first, last, _ = sent[0]
        owned = (slot_local, first, last)
        spectra = first_spectra_of(
            order_table, owned, parts, part, fields, day_block * lat_local
        )
        return spectra[0], swap(spectra, "wide")

    def exchange(spectra):
        spectra = spectra.reshape(wide_count, -1, spectra.shape[1])
        return lax.all_to_all(spectra, "wide", split_axis=0, concat_axis=0, tiled=True)

    def finish(job, after, others=(), final=None):
        part, first, last, _ = sent[job[0]]
        out = digest(
            lag_days,
            me,
            [received[index] for index in job],
            lat_table,
            rows_of(all_weights, part, first, last),
            narrow_count,
            part == 0,
            after,
        )
        sends, picks = out[:narrow_count], out[narrow_count:]
        total = combine(
            lag_days,
            me,
            rows_of(own_weights, part, first, last),
            swap(sends, "narrow"),
            others,
            final,
        )
        for parity in range(2):
            rows = slice(parity * (last - first), (parity + 1) * (last - first))
            if picks:
                picked[parity, first] = picks[0][:, rows]
        return total

    def panel_rows():
        series = jnp.stack(
            [
                jnp.concatenate([picked[k] for k in sorted(picked) if k[0] == parity], axis=1)
                for parity in range(2)
            ],
            axis=2,
        )
        series = series.reshape(days_local, slot_local, narrow_count * (ROW_DEG + 1))
        series = jnp.transpose(series, (1, 2, 0)).reshape(slot_local, -1)
        series = gather(series, "narrow")
        series = series.reshape(narrow_count, slot_local, narrow_count, ROW_DEG + 1, days_local)
        series = jnp.moveaxis(series, 0, 3).reshape(
            slot_local, narrow_count, ROW_DEG + 1, days_local * narrow_count
        )
        weights = all_weights[0].reshape(2, 3, pair_local, narrow_count, deg_local)
        weights = jnp.transpose(weights[..., : ROW_DEG + 1], (1, 2, 0, 3, 4)).reshape(
            3, slot_local, narrow_count, ROW_DEG + 1, 1
        )
        residual = series[..., LAGMAX:].astype(jnp.float32)
        for position in range(3):
            shifted = lax.dynamic_slice_in_dim(series, LAGMAX - lag_days[position], kept_days, axis=3)
            residual = residual - weights[position] * shifted.astype(jnp.float32)
        rounded = residual.astype(jnp.bfloat16)
        rows = rounded[:, :, :ROW_DEG].reshape(slot_local, narrow_count * ROW_DEG, kept_days)
        column = lax.dynamic_index_in_dim(rounded[:, :, ROW_DEG], me[0], 1, False)
        far = None if wide_count & (wide_count - 1) else gather_swap(column, 0, "wide")
        return rows, column, far

    def panel_of(rows, column, far):
        columns = gather(column, "wide", far).reshape(order_count, kept_days)
        product = lax.dot_general(
            rows, columns, (((2,), (1,)), ((), ())), preferred_element_type=jnp.float32
        )
        return product / math.sqrt(kept_days)

    spectra, received = {}, []
    if len(sent) > 2:
        first, blocks = first_exchange()
        received.append(blocks)
        spectra[1] = product(1, [first])
        spectra[1] = before = tie(spectra[1], blocks[1:])
        for index in reversed(range(2, len(sent))):
            before = spectra[index] = product(index, [before, all_weights])
        received += [exchange(spectra[index]) for index in range(1, len(sent) - 1)]
    else:
        for index in range(len(sent)):
            received.append(exchange(product(index, [])))
    done = [finish(jobs[0], [])]
    rows, column, far = panel_rows()
    if len(sent) > 2:
        received.append(exchange(tie(spectra[len(sent) - 1], done + [far])))
    panel = panel_of(rows, column, far)
    for job in jobs[1:-1]:
        done.append(finish(job, []))
    places = [sent[job[0]][:3] for job in jobs]
    variances = finish(jobs[-1], done + [panel], done, (kept_days, places))
    noise_variance = jnp.transpose(variances, (2, 0, 1))
    return (noise_variance, panel)


def solution(mesh):
    placed = (P("narrow", "wide", None), P(), P(), P(None, "narrow", "wide", None))
    return jax.shard_map(
        body,
        mesh=mesh,
        in_specs=placed,
        out_specs=(P("narrow", "wide", None), P("wide", None, "narrow")),
        check_vma=False,
    )
```

```python
import functools
import math

import jax
import jax.numpy as jnp
import numpy as np
from jax import lax
from jax.experimental import pallas as pl
from jax.experimental.pallas import tpu as pltpu
from jax.sharding import PartitionSpec as P

LAGMAX = 8
ROW_DEG = 3
VMEM = 40 * 2**20
FULL_VMEM = 64 * 2**20 - 2**17


def dft_columns(orders, longitudes):
    turns = np.arange(longitudes)[:, None] * np.arange(orders)[None, :] % longitudes
    angle = turns * (2.0 * np.pi / longitudes)
    scale = 1.0 / math.sqrt(longitudes)
    return np.stack([np.cos(angle) * scale, -np.sin(angle) * scale]).astype(jnp.bfloat16)


def lat_columns(degrees, latitudes):
    degree = np.arange(degrees)[None, :]
    odd_lat = 2 * np.arange(latitudes)[:, None] + 1
    period = 4 * latitudes
    unit = np.pi / (2 * latitudes)
    scale = math.sqrt(2.0 / latitudes)
    cosines = np.cos(degree * odd_lat % period * unit) * scale
    sines = np.sin((degree + 1) * odd_lat % period * unit) * scale
    table = np.concatenate([cosines, sines], axis=1).astype(jnp.bfloat16)
    return np.stack([table, np.zeros_like(table)])


ANY = pl.BlockSpec(memory_space=pl.ANY)
IN_HBM = pl.BlockSpec(memory_space=pltpu.HBM)
IN_VMEM = pl.BlockSpec(memory_space=pltpu.VMEM)
IN_SMEM = pl.BlockSpec(memory_space=pltpu.SMEM)


def picks_of(owned, order_ref, swapped=0):
    slot_local, first, last = owned
    slots = order_ref.shape[0]
    held = last - first
    rows = slots // slot_local * 2 * held
    column = lax.broadcasted_iota(jnp.int32, (1, rows), 1)
    owner, place = lax.div(column, 2 * held) ^ swapped, lax.rem(column, 2 * held)
    odd = (place >= held).astype(jnp.int32)
    slot = owner * slot_local + 2 * (first + place - held * odd) + odd
    here = lax.broadcasted_iota(jnp.int32, (slots, rows), 0)
    orders = jnp.broadcast_to(order_ref[...].astype(jnp.float32).reshape(1, slots), (8, slots))
    chosen = jnp.dot(
        orders,
        (here == slot).astype(jnp.float32),
        precision=lax.Precision.HIGHEST,
        preferred_element_type=jnp.float32,
    )
    return (here.astype(jnp.float32) == chosen[:1]).astype(jnp.bfloat16)


def spectra_kernel(owned, order_ref, part_ref, field_ref, *refs):
    out_ref, table_ref = refs[-2:]

    @pl.when(pl.program_id(0) == 0)
    def _():
        table_ref[...] = jnp.dot(
            part_ref[...], picks_of(owned, order_ref), preferred_element_type=jnp.float32
        ).astype(jnp.bfloat16)

    cells = jnp.dot(field_ref[...], table_ref[...], preferred_element_type=jnp.float32)
    out_ref[...] = cells.T.astype(jnp.bfloat16)


def first_spectra_kernel(owned, part, order_ref, part_hbm, field_hbm, *refs):
    outs, (part_ref, field_ref, sems) = refs[:-3], refs[-3:]
    rows, block = outs[0].shape
    tiles = block // 128
    cuts = [128 * (tiles * i // 3) for i in range(4)]
    part_copy = pltpu.make_async_copy(part_hbm.at[part], part_ref, sems.at[0])
    copies = []
    for index in range(3):
        cells = pl.ds(cuts[index], cuts[index + 1] - cuts[index])
        copies.append(
            pltpu.make_async_copy(field_hbm.at[cells], field_ref.at[cells], sems.at[index + 1])
        )
    part_copy.start()
    copies[0].start()
    picks = picks_of(owned, order_ref, lax.axis_index("wide"))
    part_copy.wait()
    for copy in copies[1:]:
        copy.start()
    table = jnp.dot(part_ref[...], picks, preferred_element_type=jnp.float32).astype(jnp.bfloat16)
    for start, stop, copy in zip(cuts, cuts[1:], copies):
        copy.wait()
        cells = jnp.dot(field_ref[start:stop], table, preferred_element_type=jnp.float32)
        cells = cells.T.astype(jnp.bfloat16)
        for hop, out_ref in enumerate(outs):
            out_ref[:, start:stop] = cells[hop * rows : (hop + 1) * rows]


def first_spectra_of(order_table, owned, parts, part, fields, block):
    lon_count = fields.shape[1]
    slot_local, first_pair, last_pair = owned
    hops = order_table.shape[0] // slot_local
    rows = 2 * (last_pair - first_pair)
    return pl.pallas_call(
        functools.partial(first_spectra_kernel, owned, part),
        in_specs=[IN_VMEM, IN_HBM, IN_HBM],
        out_specs=[IN_VMEM] * hops,
        out_shape=[jax.ShapeDtypeStruct((rows, block), jnp.bfloat16)] * hops,
        scratch_shapes=[
            pltpu.VMEM(parts.shape[1:], jnp.bfloat16),
            pltpu.VMEM((block, lon_count), jnp.bfloat16),
            pltpu.SemaphoreType.DMA((4,)),
        ],
        compiler_params=pltpu.CompilerParams(vmem_limit_bytes=FULL_VMEM),
        cost_estimate=pl.CostEstimate(
            flops=2 * hops * rows * block * lon_count,
            bytes_accessed=2 * (block * lon_count + hops * rows * (block + lon_count)),
            transcendentals=0,
        ),
    )(order_table, parts, fields)


def spectra_of(order_table, owned, parts, part, fields, block, blocks, after):
    lon_count = fields.shape[1]
    first, last = blocks
    slot_local, first_pair, last_pair = owned
    rows = order_table.shape[0] // slot_local * 2 * (last_pair - first_pair)
    cells = (last - first) * block
    cost = pl.CostEstimate(
        flops=2 * rows * cells * lon_count,
        bytes_accessed=2 * (cells * lon_count + rows * (cells + lon_count)),
        transcendentals=0,
    )
    out_shape = jax.ShapeDtypeStruct((rows, cells), jnp.bfloat16)
    params = pltpu.CompilerParams(vmem_limit_bytes=FULL_VMEM)
    return pl.pallas_call(
        functools.partial(spectra_kernel, owned),
        grid=(last - first,),
        in_specs=[
            pl.BlockSpec(order_table.shape, lambda i: (0,)),
            pl.BlockSpec((None,) + parts.shape[1:], lambda i: (part, 0, 0)),
            pl.BlockSpec((block, lon_count), lambda i: (i + first, 0)),
        ]
        + [ANY] * len(after),
        out_specs=pl.BlockSpec((rows, block), lambda i: (0, i)),
        out_shape=out_shape,
        scratch_shapes=[pltpu.VMEM((lon_count, rows), jnp.bfloat16)],
        compiler_params=params,
        cost_estimate=cost,
    )(order_table, parts, fields, *after)


def peer(me, hop, count):
    if count & (count - 1) == 0:
        return me ^ hop, me ^ hop
    return (me + hop) % count, (me - hop + count) % count


def digest_kernel(shape, lag_ref, me_ref, weight_ref, lat_hbm, *refs):
    groups, hops, narrow_count, lat_local, n_after = shape
    by_hop, blocks, refs = refs[:hops], list(refs[hops : hops + groups]), refs[hops + groups + n_after :]
    lat_ref, stage_ref, sems = refs[-3:]
    refs = refs[:-3]
    copies = []
    if len(lat_hbm.shape) == 3:
        copies.append(pltpu.make_async_copy(lat_hbm.at[0], lat_ref, sems.at[hops]))
    else:
        lat_ref = lat_hbm
    for hop, ref in enumerate(by_hop):
        source = me_ref[1] ^ hop
        copies.append(pltpu.make_async_copy(ref, stage_ref.at[source], sems.at[hop]))
    for copy in copies:
        copy.start()
    if hops:
        blocks.insert(0, stage_ref)
        for copy in copies[-hops:]:
            copy.wait()
    sends, pick_refs = refs[:narrow_count], refs[narrow_count:-3]
    line_ref, series_ref, block_ref = refs[-3:]
    days, slots, degrees = series_ref.shape
    half, padded = slots // 2, line_ref.shape[1] // 2
    start = 0
    for block in blocks:
        stop = start + block.shape[2] // lat_local
        for day in range(start, stop):
            cells = slice((day - start) * lat_local, (day - start + 1) * lat_local)
            for source in range(block.shape[0]):
                lats = slice(source * lat_local, (source + 1) * lat_local)
                if half == padded:
                    line_ref[day, :, lats] = block[source, :, cells]
                else:
                    line_ref[day, :half, lats] = block[source, :half, cells]
                    line_ref[day, padded : padded + half, lats] = block[source, half:, cells]
        if start == 0 and lat_ref is not lat_hbm:
            copies[0].wait()
        for parity in range(2):
            lines = line_ref[start:stop, parity * padded : (parity + 1) * padded, :]
            coeffs = jnp.dot(
                lines.reshape((stop - start) * padded, lat_ref.shape[0]),
                lat_ref[:, parity * degrees : (parity + 1) * degrees],
                preferred_element_type=jnp.float32,
            )
            coeffs = coeffs.astype(jnp.bfloat16).reshape(stop - start, padded, degrees)
            series_ref[start:stop, parity * half : (parity + 1) * half, :] = coeffs[:, :half]
        start = stop

    step = 16 if slots % 16 == 0 else slots
    lags = [lag_ref[i] for i in range(3)]
    deg_local = degrees // narrow_count
    for first in range(0, slots, step):
        rows = pl.ds(first, step)
        weights = [weight_ref[i, rows, :] for i in range(3)]

        def add_day(day, total):
            residual = series_ref[day, rows, :].astype(jnp.float32)
            for lag, weight in zip(lags, weights):
                residual = residual - weight * series_ref[day - lag, rows, :].astype(jnp.float32)
            return total + residual * residual

        total = lax.fori_loop(
            LAGMAX, days, add_day, jnp.zeros((step, degrees), jnp.float32), unroll=4
        )
        coarse = total.astype(jnp.bfloat16)
        fine = (total - coarse.astype(jnp.float32)).astype(jnp.bfloat16)
        for owner in range(narrow_count):
            own = slice(owner * deg_local, (owner + 1) * deg_local)
            block_ref[owner, :LAGMAX, rows, :] = series_ref[:LAGMAX, rows, own]
            block_ref[owner, LAGMAX : 2 * LAGMAX, rows, :] = series_ref[days - LAGMAX :, rows, own]
            block_ref[owner, 2 * LAGMAX, rows, :] = coarse[:, own]
            block_ref[owner, 2 * LAGMAX + 1, rows, :] = fine[:, own]
    for pick_ref in pick_refs:
        for owner in range(narrow_count):
            kept = slice(owner * (ROW_DEG + 1), (owner + 1) * (ROW_DEG + 1))
            first = owner * deg_local
            pick_ref[:, :, kept] = series_ref[:, :, first : first + ROW_DEG + 1]
    me = me_ref[0]
    for hop, send in enumerate(sends):
        send[...] = block_ref[peer(me, hop, narrow_count)[0]]


def digest(lag_days, me, received, lat_table, weights, narrow_count, wants_picks, after):
    by_hop = received[0] if isinstance(received[0], list) else []
    received = received[1:] if by_hop else received
    sources, slots, _ = received[0].shape
    latitudes, degrees = lat_table.shape[-2], lat_table.shape[-1] // 2
    lat_local = latitudes // sources
    days_local = sum(block.shape[-1] for block in by_hop[:1] + received) // lat_local
    deg_local = degrees // narrow_count
    padded = 2 * (-(-(slots // 2) // 8) * 8)
    message = (2 * LAGMAX + 2, slots, deg_local)
    picked = (days_local, slots, narrow_count * (ROW_DEG + 1))
    return pl.pallas_call(
        functools.partial(
            digest_kernel, (len(received), len(by_hop), narrow_count, lat_local, len(after))
        ),
        in_specs=[IN_SMEM, IN_SMEM, IN_VMEM, IN_HBM if lat_table.ndim == 3 else IN_VMEM]
        + [ANY] * len(by_hop)
        + [IN_VMEM] * len(received)
        + [ANY] * len(after),
        out_specs=[IN_VMEM] * (narrow_count + wants_picks),
        out_shape=[jax.ShapeDtypeStruct(message, jnp.bfloat16)] * narrow_count
        + [jax.ShapeDtypeStruct(picked, jnp.bfloat16)] * wants_picks,
        scratch_shapes=[
            pltpu.VMEM((days_local, padded, latitudes), jnp.bfloat16),
            pltpu.VMEM((days_local, slots, degrees), jnp.bfloat16),
            pltpu.VMEM((narrow_count,) + message, jnp.bfloat16),
            pltpu.VMEM(lat_table.shape[-2:] if lat_table.ndim == 3 else (16, 128), jnp.bfloat16),
            pltpu.VMEM((sources,) + by_hop[0].shape if by_hop else (8, 128), jnp.bfloat16),
            pltpu.SemaphoreType.DMA((len(by_hop) + 1,)),
        ],
        compiler_params=pltpu.CompilerParams(vmem_limit_bytes=FULL_VMEM if slots > 32 else VMEM // 2),
        cost_estimate=pl.CostEstimate(
            flops=4 * slots * days_local * latitudes * degrees,
            bytes_accessed=2 * slots * days_local * (latitudes + degrees),
            transcendentals=0,
        ),
    )(lag_days, me, weights, lat_table, *by_hop, *received, *after)


def tie(array, after):
    return pl.pallas_call(
        lambda *refs: None,
        in_specs=[ANY] * (1 + len(after)),
        out_specs=ANY,
        out_shape=jax.ShapeDtypeStruct(array.shape, array.dtype),
        input_output_aliases={0: 0},
    )(array, *after)


def hold_kernel(table_ref, *refs):
    out_ref, sem = refs[-2:]
    copy = pltpu.make_async_copy(table_ref.at[0], out_ref, sem)
    copy.start()
    copy.wait()


def hold(table, after):
    return pl.pallas_call(
        hold_kernel,
        in_specs=[ANY] * (1 + len(after)),
        out_specs=IN_VMEM,
        out_shape=jax.ShapeDtypeStruct(table.shape[1:], table.dtype),
        scratch_shapes=[pltpu.SemaphoreType.DMA(())],
        compiler_params=pltpu.CompilerParams(vmem_limit_bytes=VMEM // 2),
    )(table, *after)


def combine_kernel(count, final, lag_ref, me_ref, weight_ref, *refs):
    got, others, (out_ref, seam_ref, sum_ref) = refs[:count], refs[count:-3], refs[-3:]
    me = me_ref[0]
    total = jnp.zeros(sum_ref.shape[1:], jnp.float32)
    for hop in range(count):
        source = peer(me, hop, count)[1]
        seam_ref[source, LAGMAX:] = got[hop][:LAGMAX]
        seam_ref[source + 1, :LAGMAX] = got[hop][LAGMAX : 2 * LAGMAX]
        sums = got[hop][2 * LAGMAX :].astype(jnp.float32)
        sum_ref[source] = sums[0] + sums[1]
    for source in range(count):
        total = total + sum_ref[source]
    lags = [lag_ref[i] for i in range(3)]
    weights = [weight_ref[i] for i in range(3)]
    for block in range(1, count):
        for day in range(LAGMAX, 2 * LAGMAX):
            residual = seam_ref[block, day].astype(jnp.float32)
            for lag, weight in zip(lags, weights):
                residual = residual - weight * seam_ref[block, day - lag].astype(jnp.float32)
            total = total + residual * residual
    if final is None:
        out_ref[...] = total
        return
    sum_ref[0] = total
    kept_days, places = final
    for source, (part, first, last) in zip([*others, sum_ref.at[0]], places):
        held = last - first
        for parity in range(2):
            for pair in range(first, last):
                row = parity * held + pair - first
                out_ref[2 * pair + parity, part : part + 1, :] = (
                    source[row : row + 1, :] / kept_days
                )


def combine(lag_days, me, weights, got, others=(), final=None):
    count = len(got)
    days, slots, degrees = got[0].shape
    shape = (slots, degrees)
    if final is not None:
        shape = (2 * max(last for _, _, last in final[1]), 2, degrees)
    return pl.pallas_call(
        functools.partial(combine_kernel, count, final),
        in_specs=[IN_SMEM, IN_SMEM] + [IN_VMEM] * (count + 1 + len(others)),
        out_specs=IN_VMEM,
        out_shape=jax.ShapeDtypeStruct(shape, jnp.float32),
        scratch_shapes=[
            pltpu.VMEM((count + 1, 2 * LAGMAX, slots, degrees), jnp.bfloat16),
            pltpu.VMEM((count, slots, degrees), jnp.float32),
        ],
        compiler_params=pltpu.CompilerParams(vmem_limit_bytes=VMEM // 2),
        cost_estimate=pl.CostEstimate(
            flops=8 * count * LAGMAX * slots * degrees,
            bytes_accessed=2 * count * days * slots * degrees,
            transcendentals=0,
        ),
    )(lag_days, me, weights, *got, *others)


def swap(sends, axis):
    count = lax.axis_size(axis)
    return [sends[0]] + [
        lax.ppermute(sends[hop], axis, [(i, peer(i, hop, count)[0]) for i in range(count)])
        for hop in range(1, count)
    ]


def gather_swap(held, depth, axis):
    count = lax.axis_size(axis)
    reach = count >> (depth + 1)
    return lax.ppermute(held, axis, [(i, i ^ reach) for i in range(count)])


def gather(block, axis, other=None):
    count = lax.axis_size(axis)
    if count & (count - 1):
        return lax.all_gather(block, axis)
    held, depth = block, 0
    while count >> (depth + 1):
        if depth or other is None:
            other = gather_swap(held, depth, axis)
        upper = (lax.axis_index(axis) & (count >> (depth + 1))) != 0
        pair = [jnp.where(upper, other, held), jnp.where(upper, held, other)]
        held, depth = jnp.stack(pair, axis=depth), depth + 1
    return held.reshape((count,) + block.shape)


def plan_of(slot_local, days_local, day_block, wide_count):
    pairs, blocks = slot_local // 2, days_local // day_block
    every = (0, blocks)
    if slot_local % 48 == 0 and blocks > 1 and wide_count & (wide_count - 1) == 0:
        cut = pairs * 2 // 3
        sent = [(0, 0, pairs, (0, 1)), (0, 0, pairs, (1, blocks)), (1, 0, cut, every), (1, cut, pairs, every)]
        return sent, [(0, 1), (2,), (3,)]
    return [(0, 0, pairs, every), (1, 0, pairs, every)], [(0,), (1,)]


def body(daily_fields, order_table, lag_days, lag_weights):
    wide_count = lax.axis_size("wide")
    narrow_count = lax.axis_size("narrow")
    days_local, lat_local, lon_count = daily_fields.shape
    order_count = order_table.shape[0]
    slot_local = order_count // wide_count
    pair_local = slot_local // 2
    deg_local = lag_weights.shape[1]
    deg_count = deg_local * narrow_count
    kept_days = days_local * narrow_count - LAGMAX
    day_block = math.gcd(128 // math.gcd(128, lat_local), days_local)
    me = jnp.stack([lax.axis_index("narrow"), lax.axis_index("wide")]).astype(jnp.int32)

    fields = daily_fields.reshape(days_local * lat_local, lon_count)
    parts = jnp.asarray(dft_columns(order_count, lon_count))
    lat_table = jnp.asarray(lat_columns(deg_count, lat_local * wide_count))
    own_weights = jnp.transpose(
        lag_weights.reshape(3, deg_local, pair_local, 2, 2), (4, 3, 0, 2, 1)
    )
    all_weights = gather(own_weights, "narrow")
    all_weights = jnp.moveaxis(all_weights, 0, 4).reshape(2, 2, 3, pair_local, deg_count)

    def rows_of(weights, part, first, last):
        return jnp.concatenate([weights[part, parity, :, first:last] for parity in range(2)], axis=1)

    sent, jobs = plan_of(slot_local, days_local, day_block, wide_count)
    picked = {}

    def product(index, after):
        part, first, last, blocks = sent[index]
        owned = (slot_local, first, last)
        return spectra_of(order_table, owned, parts, part, fields, day_block * lat_local, blocks, after)

    def first_exchange():
        part, first, last, _ = sent[0]
        owned = (slot_local, first, last)
        spectra = first_spectra_of(
            order_table, owned, parts, part, fields, day_block * lat_local
        )
        return spectra[0], swap(spectra, "wide")

    def exchange(spectra):
        spectra = spectra.reshape(wide_count, -1, spectra.shape[1])
        return lax.all_to_all(spectra, "wide", split_axis=0, concat_axis=0, tiled=True)

    def finish(job, after, table, others=(), final=None):
        part, first, last, _ = sent[job[0]]
        out = digest(
            lag_days,
            me,
            [received[index] for index in job],
            table,
            rows_of(all_weights, part, first, last),
            narrow_count,
            part == 0,
            after,
        )
        sends, picks = out[:narrow_count], out[narrow_count:]
        total = combine(
            lag_days,
            me,
            rows_of(own_weights, part, first, last),
            swap(sends, "narrow"),
            others,
            final,
        )
        for parity in range(2):
            rows = slice(parity * (last - first), (parity + 1) * (last - first))
            if picks:
                picked[parity, first] = picks[0][:, rows]
        return total, sends[0]

    def panel_rows():
        series = jnp.stack(
            [
                jnp.concatenate([picked[k] for k in sorted(picked) if k[0] == parity], axis=1)
                for parity in range(2)
            ],
            axis=2,
        )
        series = series.reshape(days_local, slot_local, narrow_count * (ROW_DEG + 1))
        series = jnp.transpose(series, (1, 2, 0)).reshape(slot_local, -1)
        series = gather(series, "narrow")
        series = series.reshape(narrow_count, slot_local, narrow_count, ROW_DEG + 1, days_local)
        series = jnp.moveaxis(series, 0, 3).reshape(
            slot_local, narrow_count, ROW_DEG + 1, days_local * narrow_count
        )
        weights = all_weights[0].reshape(2, 3, pair_local, narrow_count, deg_local)
        weights = jnp.transpose(weights[..., : ROW_DEG + 1], (1, 2, 0, 3, 4)).reshape(
            3, slot_local, narrow_count, ROW_DEG + 1, 1
        )
        residual = series[..., LAGMAX:].astype(jnp.float32)
        for position in range(3):
            shifted = lax.dynamic_slice_in_dim(series, LAGMAX - lag_days[position], kept_days, axis=3)
            residual = residual - weights[position] * shifted.astype(jnp.float32)
        rounded = residual.astype(jnp.bfloat16)
        rows = rounded[:, :, :ROW_DEG].reshape(slot_local, narrow_count * ROW_DEG, kept_days)
        column = lax.dynamic_index_in_dim(rounded[:, :, ROW_DEG], me[0], 1, False)
        far = None if wide_count & (wide_count - 1) else gather_swap(column, 0, "wide")
        return rows, column, far

    def panel_of(rows, column, far):
        columns = gather(column, "wide", far).reshape(order_count, kept_days)
        product = lax.dot_general(
            rows, columns, (((2,), (1,)), ((), ())), preferred_element_type=jnp.float32
        )
        return product / math.sqrt(kept_days)

    spectra, received = {}, []
    if len(sent) > 2:
        first, blocks = first_exchange()
        received.append(blocks)
        spectra[1] = product(1, [first])
        spectra[1] = before = tie(spectra[1], blocks[1:])
        for index in reversed(range(2, len(sent))):
            before = spectra[index] = product(index, [before, all_weights])
        received += [exchange(spectra[index]) for index in range(1, len(sent) - 1)]
    else:
        for index in range(len(sent)):
            received.append(exchange(product(index, [])))
    done = [finish(jobs[0], [], lat_table)[0]]
    table = lat_table
    rows, column, far = panel_rows()
    if len(sent) > 2:
        received.append(exchange(tie(spectra[len(sent) - 1], done + [far])))
    panel = panel_of(rows, column, far)
    for job in jobs[1:-1]:
        total, message = finish(job, [], lat_table)
        table = hold(lat_table, [message])
        done.append(total)
    places = [sent[job[0]][:3] for job in jobs]
    variances, _ = finish(jobs[-1], done + [panel], table, done, (kept_days, places))
    noise_variance = jnp.transpose(variances, (2, 0, 1))
    return (noise_variance, panel)


def solution(mesh):
    placed = (P("narrow", "wide", None), P(), P(), P(None, "narrow", "wide", None))
    return jax.shard_map(
        body,
        mesh=mesh,
        in_specs=placed,
        out_specs=(P("narrow", "wide", None), P("wide", None, "narrow")),
        check_vma=False,
    )
```

```python
import functools
import math

import jax
import jax.numpy as jnp
import numpy as np
from jax import lax
from jax.experimental import pallas as pl
from jax.experimental.pallas import tpu as pltpu
from jax.sharding import PartitionSpec as P

LAGMAX = 8
ROW_DEG = 3
VMEM = 40 * 2**20
FULL_VMEM = 64 * 2**20 - 2**17


def dft_columns(orders, longitudes):
    turns = np.arange(longitudes)[:, None] * np.arange(orders)[None, :] % longitudes
    angle = turns * (2.0 * np.pi / longitudes)
    scale = 1.0 / math.sqrt(longitudes)
    return np.stack([np.cos(angle) * scale, -np.sin(angle) * scale]).astype(jnp.bfloat16)


def lat_columns(degrees, latitudes):
    degree = np.arange(degrees)[None, :]
    odd_lat = 2 * np.arange(latitudes)[:, None] + 1
    period = 4 * latitudes
    unit = np.pi / (2 * latitudes)
    scale = math.sqrt(2.0 / latitudes)
    cosines = np.cos(degree * odd_lat % period * unit) * scale
    sines = np.sin((degree + 1) * odd_lat % period * unit) * scale
    table = np.concatenate([cosines, sines], axis=1).astype(jnp.bfloat16)
    return np.stack([table, np.zeros_like(table)])


ANY = pl.BlockSpec(memory_space=pl.ANY)
IN_HBM = pl.BlockSpec(memory_space=pltpu.HBM)
IN_VMEM = pl.BlockSpec(memory_space=pltpu.VMEM)
IN_SMEM = pl.BlockSpec(memory_space=pltpu.SMEM)


def picks_of(owned, order_ref, swapped=0):
    slot_local, first, last = owned
    slots = order_ref.shape[0]
    held = last - first
    rows = slots // slot_local * 2 * held
    column = lax.broadcasted_iota(jnp.int32, (1, rows), 1)
    owner, place = lax.div(column, 2 * held) ^ swapped, lax.rem(column, 2 * held)
    odd = (place >= held).astype(jnp.int32)
    slot = owner * slot_local + 2 * (first + place - held * odd) + odd
    here = lax.broadcasted_iota(jnp.int32, (slots, rows), 0)
    orders = jnp.broadcast_to(order_ref[...].astype(jnp.float32).reshape(1, slots), (8, slots))
    chosen = jnp.dot(
        orders,
        (here == slot).astype(jnp.float32),
        precision=lax.Precision.HIGHEST,
        preferred_element_type=jnp.float32,
    )
    return (here.astype(jnp.float32) == chosen[:1]).astype(jnp.bfloat16)


def spectra_kernel(owned, order_ref, part_ref, field_ref, *refs):
    out_ref, table_ref = refs[-2:]

    @pl.when(pl.program_id(0) == 0)
    def _():
        table_ref[...] = jnp.dot(
            part_ref[...], picks_of(owned, order_ref), preferred_element_type=jnp.float32
        ).astype(jnp.bfloat16)

    cells = jnp.dot(field_ref[...], table_ref[...], preferred_element_type=jnp.float32)
    out_ref[...] = cells.T.astype(jnp.bfloat16)


def first_spectra_kernel(owned, part, order_ref, part_hbm, field_hbm, *refs):
    outs, (part_ref, field_ref, sems) = refs[:-3], refs[-3:]
    rows, block = outs[0].shape
    tiles = block // 128
    cuts = [128 * (tiles * i // 3) for i in range(4)]
    part_copy = pltpu.make_async_copy(part_hbm.at[part], part_ref, sems.at[0])
    copies = []
    for index in range(3):
        cells = pl.ds(cuts[index], cuts[index + 1] - cuts[index])
        copies.append(
            pltpu.make_async_copy(field_hbm.at[cells], field_ref.at[cells], sems.at[index + 1])
        )
    part_copy.start()
    copies[0].start()
    picks = picks_of(owned, order_ref, lax.axis_index("wide"))
    part_copy.wait()
    for copy in copies[1:]:
        copy.start()
    table = jnp.dot(part_ref[...], picks, preferred_element_type=jnp.float32).astype(jnp.bfloat16)
    for start, stop, copy in zip(cuts, cuts[1:], copies):
        copy.wait()
        cells = jnp.dot(field_ref[start:stop], table, preferred_element_type=jnp.float32)
        cells = cells.T.astype(jnp.bfloat16)
        for hop, out_ref in enumerate(outs):
            out_ref[:, start:stop] = cells[hop * rows : (hop + 1) * rows]


def first_spectra_of(order_table, owned, parts, part, fields, block):
    lon_count = fields.shape[1]
    slot_local, first_pair, last_pair = owned
    hops = order_table.shape[0] // slot_local
    rows = 2 * (last_pair - first_pair)
    return pl.pallas_call(
        functools.partial(first_spectra_kernel, owned, part),
        in_specs=[IN_VMEM, IN_HBM, IN_HBM],
        out_specs=[IN_VMEM] * hops,
        out_shape=[jax.ShapeDtypeStruct((rows, block), jnp.bfloat16)] * hops,
        scratch_shapes=[
            pltpu.VMEM(parts.shape[1:], jnp.bfloat16),
            pltpu.VMEM((block, lon_count), jnp.bfloat16),
            pltpu.SemaphoreType.DMA((4,)),
        ],
        compiler_params=pltpu.CompilerParams(vmem_limit_bytes=FULL_VMEM),
        cost_estimate=pl.CostEstimate(
            flops=2 * hops * rows * block * lon_count,
            bytes_accessed=2 * (block * lon_count + hops * rows * (block + lon_count)),
            transcendentals=0,
        ),
    )(order_table, parts, fields)


def spectra_of(order_table, owned, parts, part, fields, block, blocks, after):
    lon_count = fields.shape[1]
    first, last, skip = blocks
    last = last - skip
    slot_local, first_pair, last_pair = owned
    rows = order_table.shape[0] // slot_local * 2 * (last_pair - first_pair)
    cells = (last - first) * block
    cost = pl.CostEstimate(
        flops=2 * rows * cells * lon_count,
        bytes_accessed=2 * (cells * lon_count + rows * (cells + lon_count)),
        transcendentals=0,
    )
    out_shape = jax.ShapeDtypeStruct((rows, cells), jnp.bfloat16)
    params = pltpu.CompilerParams(vmem_limit_bytes=FULL_VMEM)
    return pl.pallas_call(
        functools.partial(spectra_kernel, owned),
        grid=(last - first,),
        in_specs=[
            pl.BlockSpec(order_table.shape, lambda i: (0,)),
            pl.BlockSpec((None,) + parts.shape[1:], lambda i: (part, 0, 0)),
            pl.BlockSpec((block, lon_count), lambda i: (i + first + (i > 0) * skip, 0)),
        ]
        + [ANY] * len(after),
        out_specs=pl.BlockSpec((rows, block), lambda i: (0, i)),
        out_shape=out_shape,
        scratch_shapes=[pltpu.VMEM((lon_count, rows), jnp.bfloat16)],
        compiler_params=params,
        cost_estimate=cost,
    )(order_table, parts, fields, *after)


def peer(me, hop, count):
    if count & (count - 1) == 0:
        return me ^ hop, me ^ hop
    return (me + hop) % count, (me - hop + count) % count


def digest_kernel(shape, lag_ref, me_ref, weight_ref, lat_hbm, *refs):
    groups, hops, narrow_count, lat_local, n_after, spans, ranges, kind = shape
    edge_refs, refs = refs[: kind == "last"], refs[kind == "last" :]
    by_hop, blocks, refs = refs[:hops], list(refs[hops : hops + groups]), refs[hops + groups + n_after :]
    lat_ref, stage_ref, sems = refs[-3:]
    refs = refs[:-3]
    copies = []
    if len(lat_hbm.shape) == 3:
        copies.append(pltpu.make_async_copy(lat_hbm.at[0], lat_ref, sems.at[hops]))
    else:
        lat_ref = lat_hbm
    for hop, ref in enumerate(by_hop):
        source = me_ref[1] ^ hop
        copies.append(pltpu.make_async_copy(ref, stage_ref.at[source], sems.at[hop]))
    for copy in copies:
        copy.start()
    if hops:
        blocks.insert(0, stage_ref)
        for copy in copies[-hops:]:
            copy.wait()
    sends, pick_refs = refs[:narrow_count], refs[narrow_count:-3]
    made_refs, pick_refs = (pick_refs, []) if kind == "edges" else ([], pick_refs)
    line_ref, series_ref, block_ref = refs[-3:]
    days, slots, degrees = series_ref.shape
    half, padded = slots // 2, line_ref.shape[1] // 2
    for edge_ref in edge_refs:
        for index, first in enumerate((spans[0][0] - LAGMAX, spans[0][1])):
            series_ref[first : first + LAGMAX] = edge_ref[index * LAGMAX : (index + 1) * LAGMAX]
    pieces = []
    for block in blocks:
        used = 0
        while used < block.shape[2] // lat_local:
            start, stop = spans[len(pieces)]
            pieces.append((block, used, start, stop))
            used += stop - start
    for block, used, start, stop in pieces:
        for day in range(start, stop):
            cells = slice((used + day - start) * lat_local, (used + day - start + 1) * lat_local)
            for source in range(block.shape[0]):
                lats = slice(source * lat_local, (source + 1) * lat_local)
                if half == padded:
                    line_ref[day, :, lats] = block[source, :, cells]
                else:
                    line_ref[day, :half, lats] = block[source, :half, cells]
                    line_ref[day, padded : padded + half, lats] = block[source, half:, cells]
        if start == spans[0][0] and lat_ref is not lat_hbm:
            copies[0].wait()
        for parity in range(2):
            lines = line_ref[start:stop, parity * padded : (parity + 1) * padded, :]
            coeffs = jnp.dot(
                lines.reshape((stop - start) * padded, lat_ref.shape[0]),
                lat_ref[:, parity * degrees : (parity + 1) * degrees],
                preferred_element_type=jnp.float32,
            )
            coeffs = coeffs.astype(jnp.bfloat16).reshape(stop - start, padded, degrees)
            series_ref[start:stop, parity * half : (parity + 1) * half, :] = coeffs[:, :half]

    step = 16 if slots % 16 == 0 else slots
    lags = [lag_ref[i] for i in range(3)]
    deg_local = degrees // narrow_count
    for first in range(0, slots, step):
        rows = pl.ds(first, step)
        weights = [weight_ref[i, rows, :] for i in range(3)]

        def add_day(day, total):
            residual = series_ref[day, rows, :].astype(jnp.float32)
            for lag, weight in zip(lags, weights):
                residual = residual - weight * series_ref[day - lag, rows, :].astype(jnp.float32)
            return total + residual * residual

        total = jnp.zeros((step, degrees), jnp.float32)
        for start, stop in ranges:
            total = lax.fori_loop(start, stop, add_day, total, unroll=4)
        coarse = total.astype(jnp.bfloat16)
        fine = (total - coarse.astype(jnp.float32)).astype(jnp.bfloat16)
        for owner in range(narrow_count):
            own = slice(owner * deg_local, (owner + 1) * deg_local)
            if kind != "last":
                block_ref[owner, :LAGMAX, rows, :] = series_ref[:LAGMAX, rows, own]
                block_ref[owner, LAGMAX : 2 * LAGMAX, rows, :] = series_ref[days - LAGMAX :, rows, own]
            block_ref[owner, block_ref.shape[1] - 2, rows, :] = coarse[:, own]
            block_ref[owner, block_ref.shape[1] - 1, rows, :] = fine[:, own]
    for made_ref in made_refs:
        for index, first in enumerate((spans[0][1] - LAGMAX, spans[1][0])):
            made_ref[index * LAGMAX : (index + 1) * LAGMAX] = series_ref[first : first + LAGMAX]
    for pick_ref in pick_refs:
        for owner in range(narrow_count):
            kept = slice(owner * (ROW_DEG + 1), (owner + 1) * (ROW_DEG + 1))
            first = owner * deg_local
            pick_ref[:, :, kept] = series_ref[:, :, first : first + ROW_DEG + 1]
    me = me_ref[0]
    for hop, send in enumerate(sends):
        send[...] = block_ref[peer(me, hop, narrow_count)[0]]


def digest(lag_days, me, received, lat_table, weights, narrow_count, days_local, spans, kind, edges, after):
    ranges = [(LAGMAX, days_local)]
    if kind == "edges":
        ranges = [(LAGMAX, spans[0][1]), (spans[1][0] + LAGMAX, days_local)]
    if kind == "last":
        ranges = [(spans[0][0], spans[0][1] + LAGMAX)]
    by_hop = received[0] if isinstance(received[0], list) else []
    received = received[1:] if by_hop else received
    sources, slots, _ = received[0].shape
    latitudes, degrees = lat_table.shape[-2], lat_table.shape[-1] // 2
    lat_local = latitudes // sources
    deg_local = degrees // narrow_count
    padded = 2 * (-(-(slots // 2) // 8) * 8)
    message = (2 if kind == "last" else 2 * LAGMAX + 2, slots, deg_local)
    extras = {
        "picks": [(days_local, slots, narrow_count * (ROW_DEG + 1))],
        "edges": [(2 * LAGMAX, slots, degrees)],
    }.get(kind, [])
    return pl.pallas_call(
        functools.partial(
            digest_kernel, (len(received), len(by_hop), narrow_count, lat_local, len(after), spans, ranges, kind)
        ),
        in_specs=[IN_SMEM, IN_SMEM, IN_VMEM, IN_HBM if lat_table.ndim == 3 else IN_VMEM]
        + [IN_VMEM] * len(edges)
        + [ANY] * len(by_hop)
        + [IN_VMEM] * len(received)
        + [ANY] * len(after),
        out_specs=[IN_VMEM] * (narrow_count + len(extras)),
        out_shape=[jax.ShapeDtypeStruct(message, jnp.bfloat16)] * narrow_count
        + [jax.ShapeDtypeStruct(shape, jnp.bfloat16) for shape in extras],
        scratch_shapes=[
            pltpu.VMEM((days_local, padded, latitudes), jnp.bfloat16),
            pltpu.VMEM((days_local, slots, degrees), jnp.bfloat16),
            pltpu.VMEM((narrow_count,) + message, jnp.bfloat16),
            pltpu.VMEM(lat_table.shape[-2:] if lat_table.ndim == 3 else (16, 128), jnp.bfloat16),
            pltpu.VMEM((sources,) + by_hop[0].shape if by_hop else (8, 128), jnp.bfloat16),
            pltpu.SemaphoreType.DMA((len(by_hop) + 1,)),
        ],
        compiler_params=pltpu.CompilerParams(vmem_limit_bytes=FULL_VMEM if kind == "picks" else VMEM // 2),
        cost_estimate=pl.CostEstimate(
            flops=4 * slots * days_local * latitudes * degrees,
            bytes_accessed=2 * slots * days_local * (latitudes + degrees),
            transcendentals=0,
        ),
    )(lag_days, me, weights, lat_table, *edges, *by_hop, *received, *after)


def tie(array, after):
    return pl.pallas_call(
        lambda *refs: None,
        in_specs=[ANY] * (1 + len(after)),
        out_specs=ANY,
        out_shape=jax.ShapeDtypeStruct(array.shape, array.dtype),
        input_output_aliases={0: 0},
    )(array, *after)


def hold_kernel(table_ref, *refs):
    out_ref, sem = refs[-2:]
    copy = pltpu.make_async_copy(table_ref.at[0], out_ref, sem)
    copy.start()
    copy.wait()


def hold(table, after):
    return pl.pallas_call(
        hold_kernel,
        in_specs=[ANY] * (1 + len(after)),
        out_specs=IN_VMEM,
        out_shape=jax.ShapeDtypeStruct(table.shape[1:], table.dtype),
        scratch_shapes=[pltpu.SemaphoreType.DMA(())],
        compiler_params=pltpu.CompilerParams(vmem_limit_bytes=VMEM // 2),
    )(table, *after)


def combine_kernel(count, final, lag_ref, me_ref, weight_ref, *refs):
    got, others, (out_ref, seam_ref, sum_ref) = refs[:count], refs[count:-3], refs[-3:]
    me = me_ref[0]
    seams = got[0].shape[0] > 2
    total = jnp.zeros(sum_ref.shape[1:], jnp.float32)
    for hop in range(count):
        source = peer(me, hop, count)[1]
        if seams:
            seam_ref[source, LAGMAX:] = got[hop][:LAGMAX]
            seam_ref[source + 1, :LAGMAX] = got[hop][LAGMAX : 2 * LAGMAX]
        sums = got[hop][got[hop].shape[0] - 2 :].astype(jnp.float32)
        sum_ref[source] = sums[0] + sums[1]
    for source in range(count):
        total = total + sum_ref[source]
    lags = [lag_ref[i] for i in range(3)]
    weights = [weight_ref[i] for i in range(3)]
    for block in range(1, count) if seams else []:
        for day in range(LAGMAX, 2 * LAGMAX):
            residual = seam_ref[block, day].astype(jnp.float32)
            for lag, weight in zip(lags, weights):
                residual = residual - weight * seam_ref[block, day - lag].astype(jnp.float32)
            total = total + residual * residual
    if final is None:
        out_ref[...] = total
        return
    kept_days, places = final
    sum_ref[0] = total
    if not seams:
        sum_ref[0] = total + others[-1][...]
        others = others[:-1]
    for source, (part, first, last) in zip([*others, sum_ref.at[0]], places):
        held = last - first
        for parity in range(2):
            for pair in range(first, last):
                row = parity * held + pair - first
                out_ref[2 * pair + parity, part : part + 1, :] = (
                    source[row : row + 1, :] / kept_days
                )


def combine(lag_days, me, weights, got, others=(), final=None):
    count = len(got)
    days, slots, degrees = got[0].shape
    shape = (slots, degrees)
    if final is not None:
        shape = (2 * max(last for _, _, last in final[1]), 2, degrees)
    return pl.pallas_call(
        functools.partial(combine_kernel, count, final),
        in_specs=[IN_SMEM, IN_SMEM] + [IN_VMEM] * (count + 1 + len(others)),
        out_specs=IN_VMEM,
        out_shape=jax.ShapeDtypeStruct(shape, jnp.float32),
        scratch_shapes=[
            pltpu.VMEM((count + 1, 2 * LAGMAX, slots, degrees), jnp.bfloat16),
            pltpu.VMEM((count, slots, degrees), jnp.float32),
        ],
        compiler_params=pltpu.CompilerParams(vmem_limit_bytes=VMEM // 2),
        cost_estimate=pl.CostEstimate(
            flops=8 * count * LAGMAX * slots * degrees,
            bytes_accessed=2 * count * days * slots * degrees,
            transcendentals=0,
        ),
    )(lag_days, me, weights, *got, *others)


def swap(sends, axis):
    count = lax.axis_size(axis)
    return [sends[0]] + [
        lax.ppermute(sends[hop], axis, [(i, peer(i, hop, count)[0]) for i in range(count)])
        for hop in range(1, count)
    ]


def gather_swap(held, depth, axis):
    count = lax.axis_size(axis)
    reach = count >> (depth + 1)
    return lax.ppermute(held, axis, [(i, i ^ reach) for i in range(count)])


def gather(block, axis, other=None):
    count = lax.axis_size(axis)
    if count & (count - 1):
        return lax.all_gather(block, axis)
    held, depth = block, 0
    while count >> (depth + 1):
        if depth or other is None:
            other = gather_swap(held, depth, axis)
        upper = (lax.axis_index(axis) & (count >> (depth + 1))) != 0
        pair = [jnp.where(upper, other, held), jnp.where(upper, held, other)]
        held, depth = jnp.stack(pair, axis=depth), depth + 1
    return held.reshape((count,) + block.shape)


def plan_of(slot_local, days_local, day_block, wide_count):
    pairs, blocks = slot_local // 2, days_local // day_block
    every = (0, blocks, 0)
    if slot_local % 16 == 0 and blocks > 2 and wide_count & (wide_count - 1) == 0:
        sent = [(0, 0, pairs, (0, 1, 0)), (0, 0, pairs, (1, blocks, 0))]
        sent += [(1, 0, pairs, (0, blocks, 1)), (1, 0, pairs, (1, 2, 0))]
        return sent, [(0, 1), (2,), (3,)]
    return [(0, 0, pairs, every), (1, 0, pairs, every)], [(0,), (1,)]


def body(daily_fields, order_table, lag_days, lag_weights):
    wide_count = lax.axis_size("wide")
    narrow_count = lax.axis_size("narrow")
    days_local, lat_local, lon_count = daily_fields.shape
    order_count = order_table.shape[0]
    slot_local = order_count // wide_count
    pair_local = slot_local // 2
    deg_local = lag_weights.shape[1]
    deg_count = deg_local * narrow_count
    kept_days = days_local * narrow_count - LAGMAX
    day_block = math.gcd(128 // math.gcd(128, lat_local), days_local)
    me = jnp.stack([lax.axis_index("narrow"), lax.axis_index("wide")]).astype(jnp.int32)

    fields = daily_fields.reshape(days_local * lat_local, lon_count)
    parts = jnp.asarray(dft_columns(order_count, lon_count))
    lat_table = jnp.asarray(lat_columns(deg_count, lat_local * wide_count))
    own_weights = jnp.transpose(
        lag_weights.reshape(3, deg_local, pair_local, 2, 2), (4, 3, 0, 2, 1)
    )
    all_weights = gather(own_weights, "narrow")
    all_weights = jnp.moveaxis(all_weights, 0, 4).reshape(2, 2, 3, pair_local, deg_count)

    def rows_of(weights, part, first, last):
        return jnp.concatenate([weights[part, parity, :, first:last] for parity in range(2)], axis=1)

    sent, jobs = plan_of(slot_local, days_local, day_block, wide_count)
    picked = {}

    def product(index, after):
        part, first, last, blocks = sent[index]
        owned = (slot_local, first, last)
        return spectra_of(order_table, owned, parts, part, fields, day_block * lat_local, blocks, after)

    def first_exchange():
        part, first, last, _ = sent[0]
        owned = (slot_local, first, last)
        spectra = first_spectra_of(
            order_table, owned, parts, part, fields, day_block * lat_local
        )
        return spectra[0], swap(spectra, "wide")

    def exchange(spectra):
        spectra = spectra.reshape(wide_count, -1, spectra.shape[1])
        return lax.all_to_all(spectra, "wide", split_axis=0, concat_axis=0, tiled=True)

    def finish(job, after, table, others=(), final=None, edges=()):
        part, first, last, (begin, end, skip) = sent[job[0]]
        spans = []
        for index in job:
            begin, end, skip = sent[index][3]
            cuts = [(begin, end)] if not skip else [(begin, begin + 1), (begin + 1 + skip, end)]
            spans += [(a * day_block, b * day_block) for a, b in cuts]
        kind = "picks" if part == 0 else "edges" if skip else "last" if edges else "sums"
        out = digest(
            lag_days,
            me,
            [received[index] for index in job],
            table,
            rows_of(all_weights, part, first, last),
            narrow_count,
            days_local,
            spans,
            kind,
            edges,
            after,
        )
        sends, extras = out[:narrow_count], out[narrow_count:]
        total = combine(
            lag_days,
            me,
            rows_of(own_weights, part, first, last),
            swap(sends, "narrow"),
            others,
            final,
        )
        for parity in range(2):
            rows = slice(parity * (last - first), (parity + 1) * (last - first))
            if part == 0:
                picked[parity, first] = extras[0][:, rows]
        return total, extras

    def panel_rows():
        series = jnp.stack(
            [
                jnp.concatenate([picked[k] for k in sorted(picked) if k[0] == parity], axis=1)
                for parity in range(2)
            ],
            axis=2,
        )
        series = series.reshape(days_local, slot_local, narrow_count * (ROW_DEG + 1))
        series = jnp.transpose(series, (1, 2, 0)).reshape(slot_local, -1)
        series = gather(series, "narrow")
        series = series.reshape(narrow_count, slot_local, narrow_count, ROW_DEG + 1, days_local)
        series = jnp.moveaxis(series, 0, 3).reshape(
            slot_local, narrow_count, ROW_DEG + 1, days_local * narrow_count
        )
        weights = all_weights[0].reshape(2, 3, pair_local, narrow_count, deg_local)
        weights = jnp.transpose(weights[..., : ROW_DEG + 1], (1, 2, 0, 3, 4)).reshape(
            3, slot_local, narrow_count, ROW_DEG + 1, 1
        )
        residual = series[..., LAGMAX:].astype(jnp.float32)
        for position in range(3):
            shifted = lax.dynamic_slice_in_dim(series, LAGMAX - lag_days[position], kept_days, axis=3)
            residual = residual - weights[position] * shifted.astype(jnp.float32)
        rounded = residual.astype(jnp.bfloat16)
        rows = rounded[:, :, :ROW_DEG].reshape(slot_local, narrow_count * ROW_DEG, kept_days)
        column = lax.dynamic_index_in_dim(rounded[:, :, ROW_DEG], me[0], 1, False)
        far = None if wide_count & (wide_count - 1) else gather_swap(column, 0, "wide")
        return rows, column, far

    def panel_of(rows, column, far):
        columns = gather(column, "wide", far).reshape(order_count, kept_days)
        product = lax.dot_general(
            rows, columns, (((2,), (1,)), ((), ())), preferred_element_type=jnp.float32
        )
        return product / math.sqrt(kept_days)

    spectra, received = {}, []
    if len(sent) > 2:
        first, blocks = first_exchange()
        received.append(blocks)
        spectra[1] = product(1, [first])
        spectra[1] = before = tie(spectra[1], blocks[1:])
        for index in reversed(range(2, len(sent))):
            before = spectra[index] = product(index, [before, all_weights])
        received += [exchange(spectra[index]) for index in range(1, len(sent) - 1)]
    else:
        for index in range(len(sent)):
            received.append(exchange(product(index, [])))
    done = [finish(jobs[0], [], lat_table)[0]]
    table = lat_table
    rows, column, far = panel_rows()
    if len(sent) > 2:
        received.append(exchange(tie(spectra[len(sent) - 1], done + [far])))
    panel = panel_of(rows, column, far)
    edges = []
    for job in jobs[1:-1]:
        total, edges = finish(job, [], lat_table)
        table = hold(lat_table, [total])
        done.append(total)
    places = [sent[job[0]][:3] for job in (jobs[0], jobs[-1])]
    variances, _ = finish(jobs[-1], done + [panel], table, done, (kept_days, places), edges)
    noise_variance = jnp.transpose(variances, (2, 0, 1))
    return (noise_variance, panel)


def solution(mesh):
    placed = (P("narrow", "wide", None), P(), P(), P(None, "narrow", "wide", None))
    return jax.shard_map(
        body,
        mesh=mesh,
        in_specs=placed,
        out_specs=(P("narrow", "wide", None), P("wide", None, "narrow")),
        check_vma=False,
    )
```

```python
import functools
import math

import jax
import jax.numpy as jnp
import numpy as np
from jax import lax
from jax.experimental import pallas as pl
from jax.experimental.pallas import tpu as pltpu
from jax.sharding import PartitionSpec as P

LAGMAX = 8
ROW_DEG = 3
VMEM = 40 * 2**20
FULL_VMEM = 64 * 2**20 - 2**17


def dft_columns(orders, longitudes):
    turns = np.arange(longitudes)[:, None] * np.arange(orders)[None, :] % longitudes
    angle = turns * (2.0 * np.pi / longitudes)
    scale = 1.0 / math.sqrt(longitudes)
    return np.stack([np.cos(angle) * scale, -np.sin(angle) * scale]).astype(jnp.bfloat16)


def lat_columns(degrees, latitudes):
    degree = np.arange(degrees)[None, :]
    odd_lat = 2 * np.arange(latitudes)[:, None] + 1
    period = 4 * latitudes
    unit = np.pi / (2 * latitudes)
    scale = math.sqrt(2.0 / latitudes)
    cosines = np.cos(degree * odd_lat % period * unit) * scale
    sines = np.sin((degree + 1) * odd_lat % period * unit) * scale
    table = np.concatenate([cosines, sines], axis=1).astype(jnp.bfloat16)
    return np.stack([table, np.zeros_like(table)])


ANY = pl.BlockSpec(memory_space=pl.ANY)
IN_HBM = pl.BlockSpec(memory_space=pltpu.HBM)
IN_VMEM = pl.BlockSpec(memory_space=pltpu.VMEM)
IN_SMEM = pl.BlockSpec(memory_space=pltpu.SMEM)


def picks_of(owned, order_ref, swapped=0):
    slot_local, first, last = owned
    slots = order_ref.shape[0]
    held = last - first
    rows = slots // slot_local * 2 * held
    column = lax.broadcasted_iota(jnp.int32, (1, rows), 1)
    owner, place = lax.div(column, 2 * held) ^ swapped, lax.rem(column, 2 * held)
    odd = (place >= held).astype(jnp.int32)
    slot = owner * slot_local + 2 * (first + place - held * odd) + odd
    here = lax.broadcasted_iota(jnp.int32, (slots, rows), 0)
    orders = jnp.broadcast_to(order_ref[...].astype(jnp.float32).reshape(1, slots), (8, slots))
    chosen = jnp.dot(
        orders,
        (here == slot).astype(jnp.float32),
        precision=lax.Precision.HIGHEST,
        preferred_element_type=jnp.float32,
    )
    return (here.astype(jnp.float32) == chosen[:1]).astype(jnp.bfloat16)


def spectra_kernel(owned, order_ref, part_ref, field_ref, *refs):
    out_ref, table_ref = refs[-2:]

    @pl.when(pl.program_id(0) == 0)
    def _():
        table_ref[...] = jnp.dot(
            part_ref[...], picks_of(owned, order_ref), preferred_element_type=jnp.float32
        ).astype(jnp.bfloat16)

    cells = jnp.dot(field_ref[...], table_ref[...], preferred_element_type=jnp.float32)
    out_ref[...] = cells.T.astype(jnp.bfloat16)


def first_spectra_kernel(owned, part, order_ref, part_hbm, field_hbm, *refs):
    outs, (part_ref, field_ref, sems) = refs[:-3], refs[-3:]
    rows, block = outs[0].shape
    tiles = block // 128
    cuts = [128 * (tiles * i // 3) for i in range(4)]
    part_copy = pltpu.make_async_copy(part_hbm.at[part], part_ref, sems.at[0])
    copies = []
    for index in range(3):
        cells = pl.ds(cuts[index], cuts[index + 1] - cuts[index])
        copies.append(
            pltpu.make_async_copy(field_hbm.at[cells], field_ref.at[cells], sems.at[index + 1])
        )
    part_copy.start()
    copies[0].start()
    picks = picks_of(owned, order_ref, lax.axis_index("wide"))
    part_copy.wait()
    for copy in copies[1:]:
        copy.start()
    table = jnp.dot(part_ref[...], picks, preferred_element_type=jnp.float32).astype(jnp.bfloat16)
    for start, stop, copy in zip(cuts, cuts[1:], copies):
        copy.wait()
        cells = jnp.dot(field_ref[start:stop], table, preferred_element_type=jnp.float32)
        cells = cells.T.astype(jnp.bfloat16)
        for hop, out_ref in enumerate(outs):
            out_ref[:, start:stop] = cells[hop * rows : (hop + 1) * rows]


def first_spectra_of(order_table, owned, parts, part, fields, block):
    lon_count = fields.shape[1]
    slot_local, first_pair, last_pair = owned
    hops = order_table.shape[0] // slot_local
    rows = 2 * (last_pair - first_pair)
    return pl.pallas_call(
        functools.partial(first_spectra_kernel, owned, part),
        in_specs=[IN_VMEM, IN_HBM, IN_HBM],
        out_specs=[IN_VMEM] * hops,
        out_shape=[jax.ShapeDtypeStruct((rows, block), jnp.bfloat16)] * hops,
        scratch_shapes=[
            pltpu.VMEM(parts.shape[1:], jnp.bfloat16),
            pltpu.VMEM((block, lon_count), jnp.bfloat16),
            pltpu.SemaphoreType.DMA((4,)),
        ],
        compiler_params=pltpu.CompilerParams(vmem_limit_bytes=FULL_VMEM),
        cost_estimate=pl.CostEstimate(
            flops=2 * hops * rows * block * lon_count,
            bytes_accessed=2 * (block * lon_count + hops * rows * (block + lon_count)),
            transcendentals=0,
        ),
    )(order_table, parts, fields)


def spectra_of(order_table, owned, parts, part, fields, block, blocks, after):
    lon_count = fields.shape[1]
    first, last, skip = blocks
    last = last - skip
    slot_local, first_pair, last_pair = owned
    rows = order_table.shape[0] // slot_local * 2 * (last_pair - first_pair)
    cells = (last - first) * block
    cost = pl.CostEstimate(
        flops=2 * rows * cells * lon_count,
        bytes_accessed=2 * (cells * lon_count + rows * (cells + lon_count)),
        transcendentals=0,
    )
    out_shape = jax.ShapeDtypeStruct((rows, cells), jnp.bfloat16)
    params = pltpu.CompilerParams(vmem_limit_bytes=FULL_VMEM)
    return pl.pallas_call(
        functools.partial(spectra_kernel, owned),
        grid=(last - first,),
        in_specs=[
            pl.BlockSpec(order_table.shape, lambda i: (0,)),
            pl.BlockSpec((None,) + parts.shape[1:], lambda i: (part, 0, 0)),
            pl.BlockSpec((block, lon_count), lambda i: (i + first + (i > 0) * skip, 0)),
        ]
        + [ANY] * len(after),
        out_specs=pl.BlockSpec((rows, block), lambda i: (0, i)),
        out_shape=out_shape,
        scratch_shapes=[pltpu.VMEM((lon_count, rows), jnp.bfloat16)],
        compiler_params=params,
        cost_estimate=cost,
    )(order_table, parts, fields, *after)


def peer(me, hop, count):
    if count & (count - 1) == 0:
        return me ^ hop, me ^ hop
    return (me + hop) % count, (me - hop + count) % count


def digest_kernel(shape, lag_ref, me_ref, weight_ref, lat_hbm, *refs):
    groups, hops, narrow_count, lat_local, n_after, spans, ranges, kind = shape
    edge_refs, refs = refs[: kind == "last"], refs[kind == "last" :]
    by_hop, blocks, refs = refs[:hops], list(refs[hops : hops + groups]), refs[hops + groups + n_after :]
    lat_ref, stage_ref, sems = refs[-3:]
    refs = refs[:-3]
    copies = []
    if len(lat_hbm.shape) == 3:
        copies.append(pltpu.make_async_copy(lat_hbm.at[0], lat_ref, sems.at[hops]))
    else:
        lat_ref = lat_hbm
    for hop, ref in enumerate(by_hop):
        source = me_ref[1] ^ hop
        copies.append(pltpu.make_async_copy(ref, stage_ref.at[source], sems.at[hop]))
    for copy in copies:
        copy.start()
    if hops:
        blocks.insert(0, stage_ref)
        for copy in copies[-hops:]:
            copy.wait()
    sends, pick_refs = refs[:narrow_count], refs[narrow_count:-3]
    made_refs, pick_refs = (pick_refs, []) if kind == "edges" else ([], pick_refs)
    line_ref, series_ref, block_ref = refs[-3:]
    days, slots, degrees = series_ref.shape
    half, padded = slots // 2, line_ref.shape[1] // 2
    for edge_ref in edge_refs:
        for index, first in enumerate((spans[0][0] - LAGMAX, spans[0][1])):
            series_ref[first : first + LAGMAX] = edge_ref[index * LAGMAX : (index + 1) * LAGMAX]
    pieces = []
    for block in blocks:
        used = 0
        while used < block.shape[2] // lat_local:
            start, stop = spans[len(pieces)]
            pieces.append((block, used, start, stop))
            used += stop - start
    for block, used, start, stop in pieces:
        for day in range(start, stop):
            cells = slice((used + day - start) * lat_local, (used + day - start + 1) * lat_local)
            for source in range(block.shape[0]):
                lats = slice(source * lat_local, (source + 1) * lat_local)
                if half == padded:
                    line_ref[day, :, lats] = block[source, :, cells]
                else:
                    line_ref[day, :half, lats] = block[source, :half, cells]
                    line_ref[day, padded : padded + half, lats] = block[source, half:, cells]
        if start == spans[0][0] and lat_ref is not lat_hbm:
            copies[0].wait()
        for parity in range(2):
            lines = line_ref[start:stop, parity * padded : (parity + 1) * padded, :]
            coeffs = jnp.dot(
                lines.reshape((stop - start) * padded, lat_ref.shape[0]),
                lat_ref[:, parity * degrees : (parity + 1) * degrees],
                preferred_element_type=jnp.float32,
            )
            coeffs = coeffs.astype(jnp.bfloat16).reshape(stop - start, padded, degrees)
            series_ref[start:stop, parity * half : (parity + 1) * half, :] = coeffs[:, :half]

    step = 16 if slots % 16 == 0 else slots
    lags = [lag_ref[i] for i in range(3)]
    deg_local = degrees // narrow_count
    for first in range(0, slots, step):
        rows = pl.ds(first, step)
        weights = [weight_ref[i, rows, :] for i in range(3)]

        def add_day(day, total):
            residual = series_ref[day, rows, :].astype(jnp.float32)
            for lag, weight in zip(lags, weights):
                residual = residual - weight * series_ref[day - lag, rows, :].astype(jnp.float32)
            return total + residual * residual

        total = jnp.zeros((step, degrees), jnp.float32)
        for start, stop in ranges:
            total = lax.fori_loop(start, stop, add_day, total, unroll=4)
        coarse = total.astype(jnp.bfloat16)
        fine = (total - coarse.astype(jnp.float32)).astype(jnp.bfloat16)
        for owner in range(narrow_count):
            own = slice(owner * deg_local, (owner + 1) * deg_local)
            if kind != "last":
                block_ref[owner, :LAGMAX, rows, :] = series_ref[:LAGMAX, rows, own]
                block_ref[owner, LAGMAX : 2 * LAGMAX, rows, :] = series_ref[days - LAGMAX :, rows, own]
            block_ref[owner, block_ref.shape[1] - 2, rows, :] = coarse[:, own]
            block_ref[owner, block_ref.shape[1] - 1, rows, :] = fine[:, own]
    for made_ref in made_refs:
        for index, first in enumerate((spans[0][1] - LAGMAX, spans[1][0])):
            made_ref[index * LAGMAX : (index + 1) * LAGMAX] = series_ref[first : first + LAGMAX]
    for pick_ref in pick_refs:
        for owner in range(narrow_count):
            kept = slice(owner * (ROW_DEG + 1), (owner + 1) * (ROW_DEG + 1))
            first = owner * deg_local
            pick_ref[:, :, kept] = series_ref[:, :, first : first + ROW_DEG + 1]
    me = me_ref[0]
    for hop, send in enumerate(sends):
        send[...] = block_ref[peer(me, hop, narrow_count)[0]]


def digest(lag_days, me, received, lat_table, weights, narrow_count, days_local, spans, kind, edges, after):
    ranges = [(LAGMAX, days_local)]
    if kind == "edges":
        ranges = [(LAGMAX, spans[0][1]), (spans[1][0] + LAGMAX, days_local)]
    if kind == "last":
        ranges = [(spans[0][0], spans[0][1] + LAGMAX)]
    by_hop = received[0] if isinstance(received[0], list) else []
    received = received[1:] if by_hop else received
    sources, slots, _ = received[0].shape
    latitudes, degrees = lat_table.shape[-2], lat_table.shape[-1] // 2
    lat_local = latitudes // sources
    deg_local = degrees // narrow_count
    padded = 2 * (-(-(slots // 2) // 8) * 8)
    message = (2 if kind == "last" else 2 * LAGMAX + 2, slots, deg_local)
    extras = {
        "picks": [(days_local, slots, narrow_count * (ROW_DEG + 1))],
        "edges": [(2 * LAGMAX, slots, degrees)],
    }.get(kind, [])
    return pl.pallas_call(
        functools.partial(
            digest_kernel, (len(received), len(by_hop), narrow_count, lat_local, len(after), spans, ranges, kind)
        ),
        in_specs=[IN_SMEM, IN_SMEM, IN_VMEM, IN_HBM if lat_table.ndim == 3 else IN_VMEM]
        + [IN_VMEM] * len(edges)
        + [ANY] * len(by_hop)
        + [IN_VMEM] * len(received)
        + [ANY] * len(after),
        out_specs=[IN_VMEM] * (narrow_count + len(extras)),
        out_shape=[jax.ShapeDtypeStruct(message, jnp.bfloat16)] * narrow_count
        + [jax.ShapeDtypeStruct(shape, jnp.bfloat16) for shape in extras],
        scratch_shapes=[
            pltpu.VMEM((days_local, padded, latitudes), jnp.bfloat16),
            pltpu.VMEM((days_local, slots, degrees), jnp.bfloat16),
            pltpu.VMEM((narrow_count,) + message, jnp.bfloat16),
            pltpu.VMEM(lat_table.shape[-2:] if lat_table.ndim == 3 else (16, 128), jnp.bfloat16),
            pltpu.VMEM((sources,) + by_hop[0].shape if by_hop else (8, 128), jnp.bfloat16),
            pltpu.SemaphoreType.DMA((len(by_hop) + 1,)),
        ],
        compiler_params=pltpu.CompilerParams(vmem_limit_bytes=FULL_VMEM if kind == "picks" else VMEM // 2),
        cost_estimate=pl.CostEstimate(
            flops=4 * slots * days_local * latitudes * degrees,
            bytes_accessed=2 * slots * days_local * (latitudes + degrees),
            transcendentals=0,
        ),
    )(lag_days, me, weights, lat_table, *edges, *by_hop, *received, *after)


def tie(array, after):
    return pl.pallas_call(
        lambda *refs: None,
        in_specs=[ANY] * (1 + len(after)),
        out_specs=ANY,
        out_shape=jax.ShapeDtypeStruct(array.shape, array.dtype),
        input_output_aliases={0: 0},
    )(array, *after)


def hold_kernel(table_ref, *refs):
    out_ref, sem = refs[-2:]
    copy = pltpu.make_async_copy(table_ref.at[0], out_ref, sem)
    copy.start()
    copy.wait()


def hold(table, after):
    return pl.pallas_call(
        hold_kernel,
        in_specs=[ANY] * (1 + len(after)),
        out_specs=IN_VMEM,
        out_shape=jax.ShapeDtypeStruct(table.shape[1:], table.dtype),
        scratch_shapes=[pltpu.SemaphoreType.DMA(())],
        compiler_params=pltpu.CompilerParams(vmem_limit_bytes=VMEM // 2),
    )(table, *after)


def combine_kernel(count, final, lag_ref, me_ref, weight_ref, *refs):
    got, others, (out_ref, seam_ref, sum_ref) = refs[:count][::-1], refs[count:-3], refs[-3:]
    me = me_ref[0]
    seams = got[0].shape[0] > 2
    total = jnp.zeros(sum_ref.shape[1:], jnp.float32)
    for hop in range(count):
        source = peer(me, hop, count)[1]
        if seams:
            seam_ref[source, LAGMAX:] = got[hop][:LAGMAX]
            seam_ref[source + 1, :LAGMAX] = got[hop][LAGMAX : 2 * LAGMAX]
        sums = got[hop][got[hop].shape[0] - 2 :].astype(jnp.float32)
        sum_ref[source] = sums[0] + sums[1]
    for source in range(count):
        total = total + sum_ref[source]
    lags = [lag_ref[i] for i in range(3)]
    weights = [weight_ref[i] for i in range(3)]
    for block in range(1, count) if seams else []:
        for day in range(LAGMAX, 2 * LAGMAX):
            residual = seam_ref[block, day].astype(jnp.float32)
            for lag, weight in zip(lags, weights):
                residual = residual - weight * seam_ref[block, day - lag].astype(jnp.float32)
            total = total + residual * residual
    if final is None:
        out_ref[...] = total
        return
    kept_days, places = final
    sum_ref[0] = total
    if not seams:
        sum_ref[0] = total + others[-1][...]
        others = others[:-1]
    for source, (part, first, last) in zip([*others, sum_ref.at[0]], places):
        held = last - first
        for parity in range(2):
            for pair in range(first, last):
                row = parity * held + pair - first
                out_ref[2 * pair + parity, part : part + 1, :] = (
                    source[row : row + 1, :] / kept_days
                )


def combine(lag_days, me, weights, got, others=(), final=None):
    count = len(got)
    days, slots, degrees = got[0].shape
    shape = (slots, degrees)
    if final is not None:
        shape = (2 * max(last for _, _, last in final[1]), 2, degrees)
    return pl.pallas_call(
        functools.partial(combine_kernel, count, final),
        in_specs=[IN_SMEM, IN_SMEM] + [IN_VMEM] * (count + 1 + len(others)),
        out_specs=IN_VMEM,
        out_shape=jax.ShapeDtypeStruct(shape, jnp.float32),
        scratch_shapes=[
            pltpu.VMEM((count + 1, 2 * LAGMAX, slots, degrees), jnp.bfloat16),
            pltpu.VMEM((count, slots, degrees), jnp.float32),
        ],
        compiler_params=pltpu.CompilerParams(vmem_limit_bytes=VMEM // 2),
        cost_estimate=pl.CostEstimate(
            flops=8 * count * LAGMAX * slots * degrees,
            bytes_accessed=2 * count * days * slots * degrees,
            transcendentals=0,
        ),
    )(lag_days, me, weights, *got[::-1], *others)


def swap(sends, axis):
    count = lax.axis_size(axis)
    return [sends[0]] + [
        lax.ppermute(sends[hop], axis, [(i, peer(i, hop, count)[0]) for i in range(count)])
        for hop in range(1, count)
    ]


def gather_swap(held, depth, axis):
    count = lax.axis_size(axis)
    reach = count >> (depth + 1)
    return lax.ppermute(held, axis, [(i, i ^ reach) for i in range(count)])


def gather(block, axis, other=None):
    count = lax.axis_size(axis)
    if count & (count - 1):
        return lax.all_gather(block, axis)
    held, depth = block, 0
    while count >> (depth + 1):
        if depth or other is None:
            other = gather_swap(held, depth, axis)
        upper = (lax.axis_index(axis) & (count >> (depth + 1))) != 0
        pair = [jnp.where(upper, other, held), jnp.where(upper, held, other)]
        held, depth = jnp.stack(pair, axis=depth), depth + 1
    return held.reshape((count,) + block.shape)


def plan_of(slot_local, days_local, day_block, wide_count):
    pairs, blocks = slot_local // 2, days_local // day_block
    every = (0, blocks, 0)
    if slot_local % 16 == 0 and blocks > 2 and wide_count & (wide_count - 1) == 0:
        sent = [(0, 0, pairs, (0, 1, 0)), (0, 0, pairs, (1, blocks, 0))]
        sent += [(1, 0, pairs, (0, blocks, 1)), (1, 0, pairs, (1, 2, 0))]
        return sent, [(0, 1), (2,), (3,)]
    return [(0, 0, pairs, every), (1, 0, pairs, every)], [(0,), (1,)]


def body(daily_fields, order_table, lag_days, lag_weights):
    wide_count = lax.axis_size("wide")
    narrow_count = lax.axis_size("narrow")
    days_local, lat_local, lon_count = daily_fields.shape
    order_count = order_table.shape[0]
    slot_local = order_count // wide_count
    pair_local = slot_local // 2
    deg_local = lag_weights.shape[1]
    deg_count = deg_local * narrow_count
    kept_days = days_local * narrow_count - LAGMAX
    day_block = math.gcd(128 // math.gcd(128, lat_local), days_local)
    me = jnp.stack([lax.axis_index("narrow"), lax.axis_index("wide")]).astype(jnp.int32)

    fields = daily_fields.reshape(days_local * lat_local, lon_count)
    parts = jnp.asarray(dft_columns(order_count, lon_count))
    lat_table = jnp.asarray(lat_columns(deg_count, lat_local * wide_count))
    own_weights = jnp.transpose(
        lag_weights.reshape(3, deg_local, pair_local, 2, 2), (4, 3, 0, 2, 1)
    )
    all_weights = gather(own_weights, "narrow")
    all_weights = jnp.moveaxis(all_weights, 0, 4).reshape(2, 2, 3, pair_local, deg_count)

    def rows_of(weights, part, first, last):
        return jnp.concatenate([weights[part, parity, :, first:last] for parity in range(2)], axis=1)

    sent, jobs = plan_of(slot_local, days_local, day_block, wide_count)
    picked = {}

    def product(index, after):
        part, first, last, blocks = sent[index]
        owned = (slot_local, first, last)
        return spectra_of(order_table, owned, parts, part, fields, day_block * lat_local, blocks, after)

    def first_exchange():
        part, first, last, _ = sent[0]
        owned = (slot_local, first, last)
        spectra = first_spectra_of(
            order_table, owned, parts, part, fields, day_block * lat_local
        )
        return spectra[0], swap(spectra, "wide")

    def exchange(spectra):
        spectra = spectra.reshape(wide_count, -1, spectra.shape[1])
        return lax.all_to_all(spectra, "wide", split_axis=0, concat_axis=0, tiled=True)

    def finish(job, after, table, others=(), final=None, edges=()):
        part, first, last, (begin, end, skip) = sent[job[0]]
        spans = []
        for index in job:
            begin, end, skip = sent[index][3]
            cuts = [(begin, end)] if not skip else [(begin, begin + 1), (begin + 1 + skip, end)]
            spans += [(a * day_block, b * day_block) for a, b in cuts]
        kind = "picks" if part == 0 else "edges" if skip else "last" if edges else "sums"
        out = digest(
            lag_days,
            me,
            [received[index] for index in job],
            table,
            rows_of(all_weights, part, first, last),
            narrow_count,
            days_local,
            spans,
            kind,
            edges,
            after,
        )
        sends, extras = out[:narrow_count], out[narrow_count:]
        total = combine(
            lag_days,
            me,
            rows_of(own_weights, part, first, last),
            swap(sends, "narrow"),
            others,
            final,
        )
        for parity in range(2):
            rows = slice(parity * (last - first), (parity + 1) * (last - first))
            if part == 0:
                picked[parity, first] = extras[0][:, rows]
        return total, extras

    def panel_rows():
        series = jnp.stack(
            [
                jnp.concatenate([picked[k] for k in sorted(picked) if k[0] == parity], axis=1)
                for parity in range(2)
            ],
            axis=2,
        )
        series = series.reshape(days_local, slot_local, narrow_count * (ROW_DEG + 1))
        series = jnp.transpose(series, (1, 2, 0)).reshape(slot_local, -1)
        series = gather(series, "narrow")
        series = series.reshape(narrow_count, slot_local, narrow_count, ROW_DEG + 1, days_local)
        series = jnp.moveaxis(series, 0, 3).reshape(
            slot_local, narrow_count, ROW_DEG + 1, days_local * narrow_count
        )
        weights = all_weights[0].reshape(2, 3, pair_local, narrow_count, deg_local)
        weights = jnp.transpose(weights[..., : ROW_DEG + 1], (1, 2, 0, 3, 4)).reshape(
            3, slot_local, narrow_count, ROW_DEG + 1, 1
        )
        residual = series[..., LAGMAX:].astype(jnp.float32)
        for position in range(3):
            shifted = lax.dynamic_slice_in_dim(series, LAGMAX - lag_days[position], kept_days, axis=3)
            residual = residual - weights[position] * shifted.astype(jnp.float32)
        rounded = residual.astype(jnp.bfloat16)
        rows = rounded[:, :, :ROW_DEG].reshape(slot_local, narrow_count * ROW_DEG, kept_days)
        column = lax.dynamic_index_in_dim(rounded[:, :, ROW_DEG], me[0], 1, False)
        far = None if wide_count & (wide_count - 1) else gather_swap(column, 0, "wide")
        return rows, column, far

    def panel_of(rows, column, far):
        columns = gather(column, "wide", far).reshape(order_count, kept_days)
        product = lax.dot_general(
            rows, columns, (((2,), (1,)), ((), ())), preferred_element_type=jnp.float32
        )
        return product / math.sqrt(kept_days)

    spectra, received = {}, []
    if len(sent) > 2:
        first, blocks = first_exchange()
        received.append(blocks)
        spectra[1] = product(1, [first])
        spectra[1] = before = tie(spectra[1], blocks[1:])
        for index in reversed(range(2, len(sent))):
            before = spectra[index] = product(index, [before, all_weights])
        received += [exchange(spectra[index]) for index in range(1, len(sent) - 1)]
    else:
        for index in range(len(sent)):
            received.append(exchange(product(index, [])))
    done = [finish(jobs[0], [], lat_table)[0]]
    table = lat_table
    rows, column, far = panel_rows()
    if len(sent) > 2:
        received.append(exchange(tie(spectra[len(sent) - 1], done + [far])))
    panel = panel_of(rows, column, far)
    edges = []
    for job in jobs[1:-1]:
        total, edges = finish(job, [], lat_table)
        table = hold(lat_table, [total])
        done.append(total)
    places = [sent[job[0]][:3] for job in (jobs[0], jobs[-1])]
    variances, _ = finish(jobs[-1], done + [panel], table, done, (kept_days, places), edges)
    noise_variance = jnp.transpose(variances, (2, 0, 1))
    return (noise_variance, panel)


def solution(mesh):
    placed = (P("narrow", "wide", None), P(), P(), P(None, "narrow", "wide", None))
    return jax.shard_map(
        body,
        mesh=mesh,
        in_specs=placed,
        out_specs=(P("narrow", "wide", None), P("wide", None, "narrow")),
        check_vma=False,
    )
```
